32 devices in a mesh: seq: 8 (over y, x, core), mlp: 4 (over z).
Axes of the slice: x: 2, y: 2, z: 4, core: 2. Of those that a mesh axis runs over, the one named last changes fastest.
Arguments:
- query_rows: bfloat16 [2048, 8192], P('seq'), may hold values from -256 to 256
- key_rows: bfloat16 [2048, 1024], P(('seq', 'mlp')), may hold values from -6 to 6
- value_rows: bfloat16 [2048, 1024], P(('seq', 'mlp')), may hold values from -6 to 6
- key_blocks: int32 [64, 32, 16], P(None, 'seq'), may hold values from -1 to 31, as said below
Outputs:
- attention: bfloat16 [2048, 8192], P('seq', 'mlp')
The draws below stay inside these ranges and needn't reach their ends.
Inputs may be any that keep to these rules, and one draw needn't show every extreme that they name: `key_blocks`: the list of head h and query block r names distinct blocks from 0 to r, always r itself, and holds -1 in its remaining slots; how many blocks a list names differs from head to head, and the longest list names exactly 16.
All inputs are finite; a program needn't handle non-finite values.
Results may differ from the reference program's by a relative error of at most 0.0075.
Values may be sent and summed in bfloat16 or wider, within the bound.
A program may use at most 128 MiB of HBM per device.

```python
import math
import jax
import jax.numpy as jnp
from jax import lax

H = 64
KVH = 8
HD = 128
BLK = 64
TOKENS = 2048
KMAX = 16


def draw_both(key):
    base = jax.random.fold_in(key, 11)
    second = jax.random.fold_in(base, 1)
    fourth = jax.random.fold_in(base, 3)
    key_rows = jax.random.truncated_normal(second, -6.0, 6.0, (TOKENS, KVH * HD))
    query_rows = jax.random.truncated_normal(fourth, -6.0, 6.0, (TOKENS, H * HD))
    return (query_rows, key_rows)


def draw_query_rows(key, part):
    return draw_both(key)[0].astype(jnp.bfloat16)


def draw_key_rows(key, part):
    return draw_both(key)[1].astype(jnp.bfloat16)


def draw_key_blocks(key, part):
    block_count = TOKENS // BLK
    first, second, third = jax.random.split(key, 3)
    caps = jax.random.randint(first, (H,), 1, KMAX + 1)
    densest = jax.random.randint(second, (), 0, H)
    caps = jnp.where(jnp.arange(H) == densest, KMAX, caps)
    block_rows = jnp.arange(block_count, dtype=jnp.int32)
    counts = jnp.minimum(block_rows[None, :] + 1, caps[:, None])
    random_scores = jax.random.randint(third, (H, block_count, block_count), 0, 1 << 20)
    keyed = random_scores * block_count + block_rows[None, None, :]
    keyed = jnp.where(block_rows[None, None, :] < block_rows[None, :, None], keyed, -1)
    keyed = jnp.where(block_rows[None, None, :] == block_rows[None, :, None], 2147483647, keyed)
    picked_values, picked = lax.top_k(keyed, KMAX)
    slots = jnp.arange(KMAX, dtype=jnp.int32)
    return jnp.where(slots[None, None, :] < counts[:, :, None], picked.astype(jnp.int32), -1)


def level_of(rng, shape, shards, low, largest):
    gain, own = 1.0, jax.random.fold_in(rng, 6)
    for dim, blocks in shards:
        draws = jnp.exp(jax.random.uniform(jax.random.fold_in(own, dim), (blocks,), jnp.float32, low / len(shards), largest / len(shards)))
        gain = gain * jnp.repeat(draws, shape[dim] // blocks).reshape([-1 if axis == dim else 1 for axis in range(len(shape))])
    return gain


def bell_draw(rng, extent, scale, bound, shards=(), held_as=jnp.bfloat16):
    loudness = level_of(rng, extent, shards, -0.22, 0.18) if shards else 1.0
    drawn = jax.random.normal(rng, extent, jnp.float32) * scale * loudness
    return jnp.minimum(jnp.maximum(drawn, -bound), bound).astype(held_as)


def setup_inputs(seed: int = 0) -> dict:
    arg_keys = jax.random.split(jax.random.key(seed), 5)
    query_rows = draw_query_rows(jax.random.fold_in(arg_keys[4], 71), 0)
    key_rows = draw_key_rows(jax.random.fold_in(arg_keys[4], 71), 0)
    value_rows = bell_draw(arg_keys[2], (TOKENS, KVH * HD), 1.0, 6.0, ((0, 32),))
    key_blocks = draw_key_blocks(jax.random.fold_in(arg_keys[4], 71), 0)
    return dict(query_rows=query_rows, key_rows=key_rows, value_rows=value_rows, key_blocks=key_blocks)


def reference(query_rows, key_rows, value_rows, key_blocks):
    block_count = TOKENS // BLK
    per_group = H // KVH
    score_scale = 1.0 / math.sqrt(HD)
    positions = jnp.arange(TOKENS, dtype=jnp.int32)
    causal = positions[None, :] <= positions[:, None]
    block_ids = jnp.arange(block_count, dtype=jnp.int32)

    def one_head(head):
        group = head // per_group
        query_head = lax.dynamic_slice_in_dim(query_rows, head * HD, HD, 1)
        key_head = lax.dynamic_slice_in_dim(key_rows, group * HD, HD, 1)
        value_head = lax.dynamic_slice_in_dim(value_rows, group * HD, HD, 1)
        listing = lax.dynamic_index_in_dim(key_blocks, head, 0, keepdims=False)
        named_blocks = jnp.any(listing[:, :, None] == block_ids[None, None, :], axis=1)
        allowed = jnp.repeat(jnp.repeat(named_blocks, BLK, axis=0), BLK, axis=1) & causal
        scores = jnp.dot(query_head, key_head.T, preferred_element_type=jnp.float32) * score_scale
        masked = jnp.where(allowed, scores, jnp.float32(-1e+30))
        row_max = lax.optimization_barrier(jnp.max(masked, axis=1))
        probs = jnp.where(allowed, jnp.exp(masked - row_max[:, None]), jnp.float32(0.0))
        numerator = jnp.dot(probs.astype(jnp.bfloat16), value_head, preferred_element_type=jnp.float32)
        normalizer = lax.optimization_barrier(jnp.sum(probs, axis=1))
        return (numerator / normalizer[:, None]).astype(jnp.bfloat16)
    result = lax.map(one_head, jnp.arange(H, dtype=jnp.int32))
    return jnp.transpose(result, (1, 0, 2)).reshape(TOKENS, H * HD)
```

```python
import functools
import math

import jax
import jax.numpy as jnp
from jax import lax
from jax.experimental import pallas as pl
from jax.experimental.pallas import tpu as pltpu
from jax.sharding import PartitionSpec as P

H = 64
KVH = 8
HD = 128
BLK = 64
PER_GROUP = H // KVH

MESH = pl.DeviceIdType.MESH
MASKED = -1e30
FAR = 1e9


def kernel(
    n_seq, n_mlp, list_s, list_v, q_hbm, k_hbm, v_hbm, out_ref,
    kbuf, vbuf, qbuf, kpos, probs, norm,
    local_sem, z_send, z_recv, hop_send, hop_recv, relay_send, own_sib_send, sib_send, sib_recv,
):
    s = lax.axis_index("seq")
    m = lax.axis_index("mlp")
    chips = n_seq // 2
    p, c = s // 2, s % 2
    piece = k_hbm.shape[0]
    rows = piece * n_mlp
    width = kbuf.shape[2]
    heads = H // n_mlp
    kmax = list_s.shape[2]
    q_blocks = rows // BLK
    srcs = (k_hbm, v_hbm)
    bufs = (kbuf, vbuf)
    sibling = 2 * p + 1 - c

    def piece_rows(src_s, z):
        return src_s * n_mlp + z

    def columns(z):
        return pl.ds(pl.multiple_of(z * width, width), width)

    def z_copy(a, to):
        return pltpu.make_async_remote_copy(
            src_ref=srcs[a].at[:, columns(to)], dst_ref=bufs[a].at[piece_rows(s, m)],
            send_sem=z_send.at[a, to], recv_sem=z_recv.at[a, m],
            device_id=(s, to), device_id_type=MESH)

    def z_arrival(a, z):
        return pltpu.make_async_remote_copy(
            src_ref=srcs[a].at[:, columns(z)], dst_ref=bufs[a].at[piece_rows(s, z)],
            send_sem=z_send.at[a, z], recv_sem=z_recv.at[a, z],
            device_id=(s, z), device_id_type=MESH)

    def moved(a, src_p, src_c, z, to_s, send, recv):
        part = bufs[a].at[piece_rows(2 * src_p + src_c, z)]
        return pltpu.make_async_remote_copy(
            src_ref=part, dst_ref=part, send_sem=send, recv_sem=recv,
            device_id=(to_s, m), device_id_type=MESH)

    def own_copy(a, z, to_p):
        return moved(a, p, c, z, 2 * to_p + c, hop_send.at[a, z, to_p], hop_recv.at[a, z, p])

    def hop_arrival(a, z, src_p):
        return moved(a, src_p, c, z, 2 * src_p + c, hop_send.at[a, z, src_p], hop_recv.at[a, z, src_p])

    def relay_copy(a, z, src_p, to_p):
        return moved(a, src_p, c, z, 2 * to_p + c, relay_send.at[a, z], hop_recv.at[a, z, src_p])

    def own_sib_copy(a, z):
        return moved(a, p, c, z, sibling, own_sib_send.at[a, z], sib_recv.at[a, z, p])

    def sib_copy(a, z, src_p):
        return moved(a, src_p, c, z, sibling, sib_send.at[a, z, src_p], sib_recv.at[a, z, src_p])

    def sib_arrival(a, z, src_p):
        return moved(a, src_p, 1 - c, z, sibling, sib_send.at[a, z, src_p], sib_recv.at[a, z, src_p])

    def relays(src_p):
        if chips != 4:
            return []
        zero = jnp.logical_and(src_p == 0, jnp.logical_or(
            jnp.logical_and(p == 1, c == 0), jnp.logical_and(p == 2, c == 1)))
        one = jnp.logical_and(src_p == 1, p == 3)
        return [(zero, 3), (one, 2)]

    def direct(to_p):
        if chips != 4:
            return to_p >= 0
        return jnp.logical_not(jnp.logical_or(
            jnp.logical_and(p == 0, to_p == 3), jnp.logical_and(p == 1, to_p == 2)))

    def send_own(a, z):
        @pl.loop(p + 1, chips)
        def _(to_p):
            @pl.when(direct(to_p))
            def _():
                own_copy(a, z, to_p).start()

        @pl.when(c == 0)
        def _():
            own_sib_copy(a, z).start()

    def pass_on(a, z, src_p):
        hop_arrival(a, z, src_p).wait_recv()
        for wanted, to_p in relays(src_p):
            @pl.when(wanted)
            def _():
                relay_copy(a, z, src_p, to_p).start()
        sib_copy(a, z, src_p).start()

    def z_order(i):
        return lax.rem(m + i, n_mlp)

    def local_copy(a):
        return pltpu.make_async_copy(
            srcs[a].at[:, columns(m)], bufs[a].at[piece_rows(s, m)], local_sem.at[a])

    q_copy = pltpu.make_async_copy(
        q_hbm.at[:, pl.ds(pl.multiple_of(m * heads * HD, heads * HD), heads * HD)], qbuf, local_sem.at[2])
    local_copy(0).start()
    local_copy(1).start()
    q_copy.start()

    barrier = pltpu.get_barrier_semaphore()

    @pl.loop(1, n_mlp)
    def _(i):
        pl.semaphore_signal(barrier, inc=1, device_id=(s, z_order(i)), device_id_type=MESH)

    @pl.loop(1, chips)
    def _(i):
        pl.semaphore_signal(
            barrier, inc=1, device_id=(2 * lax.rem(p + i, chips) + c, m), device_id_type=MESH)

    pl.semaphore_signal(barrier, inc=1, device_id=(sibling, m), device_id_type=MESH)
    pl.semaphore_wait(barrier, n_mlp - 1 + chips - 1 + 1)

    for a in range(2):
        @pl.loop(1, n_mlp)
        def _(i):
            z_copy(a, z_order(i)).start()

    for a in range(2):
        local_copy(a).wait()
        send_own(a, m)
        if a == 0:
            spread = (lax.broadcasted_iota(jnp.int32, (kmax, kmax * BLK), 1) // BLK
                      == lax.broadcasted_iota(jnp.int32, (kmax, kmax * BLK), 0)).astype(jnp.bfloat16)
            inside = (lax.broadcasted_iota(jnp.int32, (q_blocks, kmax * BLK), 1) % BLK).astype(jnp.float32)

            @pl.loop(0, heads)
            def _(h):
                named = list_v[m * heads + h].astype(jnp.float32).astype(jnp.bfloat16)
                block = jnp.dot(named, spread, preferred_element_type=jnp.float32)
                kpos[h] = jnp.where(block < 0, FAR, block * BLK + inside)

        @pl.loop(1, n_mlp)
        def _(i):
            z = z_order(i)
            z_arrival(a, z).wait_recv()
            send_own(a, z)

    @pl.loop(0, p * n_mlp)
    def _(i):
        pass_on(0, lax.rem(i, n_mlp), i // n_mlp)

    def finish(a):
        @pl.loop(0, (p + c) * n_mlp)
        def _(i):
            sib_arrival(a, lax.rem(i, n_mlp), i // n_mlp).wait_recv()

    finish(0)
    q_copy.wait()

    factor = math.log2(math.e) / math.sqrt(HD)
    first = s * rows
    per_head = -(-(chips - 1) * n_mlp // heads)

    def lanes(index, size):
        return pl.ds(pl.multiple_of(index * size, size), size)

    def gathered(buf, h, qb):
        group = lanes(h // PER_GROUP, HD)
        parts = []
        for k in range(kmax):
            block = jnp.maximum(list_s[m * heads + h, qb, k], 0)
            parts.append(buf[block, :, group])
        return jnp.concatenate(parts, axis=0)

    @pl.loop(0, heads)
    def _(h):
        for j in range(per_head):
            i = h * per_head + j

            @pl.when(i < p * n_mlp)
            def _():
                pass_on(1, lax.rem(i, n_mlp), i // n_mlp)

        positions = kpos[h]
        for qb in range(q_blocks):
            queries = qbuf[qb * BLK:(qb + 1) * BLK, lanes(h, HD)]
            scores = lax.dot_general(
                queries, gathered(kbuf, h, qb), (((1,), (1,)), ((), ())),
                preferred_element_type=jnp.float32)
            row = (lax.broadcasted_iota(jnp.int32, (BLK, 1), 0) + (first + qb * BLK)).astype(jnp.float32)
            scores = jnp.where(positions[qb:qb + 1, :] <= row, scores, MASKED)
            top = jnp.max(scores, axis=1, keepdims=True)
            weights = jnp.exp2((scores - top) * factor)
            total = jnp.sum(weights, axis=1, keepdims=True)
            probs[h, qb * BLK:(qb + 1) * BLK, :] = weights.astype(jnp.bfloat16)
            norm[h, qb * BLK:(qb + 1) * BLK, :] = jnp.broadcast_to(total, (BLK, HD))

    finish(1)

    @pl.loop(0, heads)
    def _(h):
        for qb in range(q_blocks):
            part = slice(qb * BLK, (qb + 1) * BLK)
            product = jnp.dot(probs[h, part, :], gathered(vbuf, h, qb), preferred_element_type=jnp.float32)
            out_ref[part, lanes(h, HD)] = (product / norm[h, part, :]).astype(out_ref.dtype)

    for a in range(2):
        @pl.loop(1, n_mlp)
        def _(i):
            z_copy(a, z_order(i)).wait_send()

        @pl.loop(0, n_mlp)
        def _(z):
            @pl.loop(p + 1, chips)
            def _(to_p):
                @pl.when(direct(to_p))
                def _():
                    own_copy(a, z, to_p).wait_send()

            @pl.when(c == 0)
            def _():
                own_sib_copy(a, z).wait_send()

            @pl.loop(0, p)
            def _(src_p):
                for wanted, to_p in relays(src_p):
                    @pl.when(wanted)
                    def _():
                        relay_copy(a, z, src_p, to_p).wait_send()
                sib_copy(a, z, src_p).wait_send()


def body(n_seq, n_mlp, query_rows, key_rows, value_rows, key_blocks):
    piece = key_rows.shape[0]
    rows = query_rows.shape[0]
    tokens = rows * n_seq
    heads = H // n_mlp
    width = (KVH // n_mlp) * HD
    kmax = key_blocks.shape[2]
    chips = n_seq // 2
    dma = pltpu.SemaphoreType.DMA
    return pl.pallas_call(
        functools.partial(kernel, n_seq, n_mlp),
        out_shape=jax.ShapeDtypeStruct((rows, heads * HD), jnp.bfloat16),
        in_specs=[
            pl.BlockSpec(memory_space=pltpu.SMEM),
            pl.BlockSpec(memory_space=pltpu.VMEM),
            pl.BlockSpec(memory_space=pl.ANY),
            pl.BlockSpec(memory_space=pl.ANY),
            pl.BlockSpec(memory_space=pl.ANY),
        ],
        out_specs=pl.BlockSpec(memory_space=pltpu.VMEM),
        scratch_shapes=[
            pltpu.VMEM((tokens // BLK, BLK, width), jnp.bfloat16),
            pltpu.VMEM((tokens // BLK, BLK, width), jnp.bfloat16),
            pltpu.VMEM((rows, heads * HD), jnp.bfloat16),
            pltpu.VMEM((heads, rows // BLK, kmax * BLK), jnp.float32),
            pltpu.VMEM((heads, rows, kmax * BLK), jnp.bfloat16),
            pltpu.VMEM((heads, rows, HD), jnp.float32),
            dma((3,)),
            dma((2, n_mlp)),
            dma((2, n_mlp)),
            dma((2, n_mlp, chips)),
            dma((2, n_mlp, chips)),
            dma((2, n_mlp)),
            dma((2, n_mlp)),
            dma((2, n_mlp, chips)),
            dma((2, n_mlp, chips)),
        ],
        compiler_params=pltpu.CompilerParams(
            collective_id=0, has_side_effects=True, vmem_limit_bytes=58 * 1024 * 1024),
        name="block_sparse_attention",
    )(key_blocks, key_blocks, query_rows, key_rows, value_rows)


def solution(mesh):
    placed = (
        P("seq", None),
        P(("seq", "mlp"), None),
        P(("seq", "mlp"), None),
        P(None, "seq", None),
    )
    return jax.shard_map(
        functools.partial(body, mesh.shape["seq"], mesh.shape["mlp"]),
        mesh=mesh, in_specs=placed, out_specs=P("seq", "mlp"), check_vma=False
    )
```

```python
import functools
import math

import jax
import jax.numpy as jnp
from jax import lax
from jax.experimental import pallas as pl
from jax.experimental.pallas import tpu as pltpu
from jax.sharding import PartitionSpec as P

H = 64
KVH = 8
HD = 128
BLK = 64
PER_GROUP = H // KVH

MESH = pl.DeviceIdType.MESH
MASKED = -1e30
FAR = 1e9


def gather_kernel(
    n_seq, n_mlp, list_v, k_hbm, v_hbm, kv, kpos, own_list, used,
    local_sem, z_send, z_recv, hop_send, hop_recv, own_sib_send, sib_send, sib_recv,
):
    s = lax.axis_index("seq")
    m = lax.axis_index("mlp")
    chips = n_seq // 2
    p, c = s // 2, s % 2
    width = kv.shape[3]
    heads, q_blocks, kmax = own_list.shape
    srcs = (k_hbm, v_hbm)
    sibling = 2 * p + 1 - c

    def columns(z):
        return pl.ds(pl.multiple_of(z * width, width), width)

    def z_copy(a, to):
        return pltpu.make_async_remote_copy(
            src_ref=srcs[a].at[:, columns(to)], dst_ref=kv.at[s * n_mlp + m, a],
            send_sem=z_send.at[a, to], recv_sem=z_recv.at[a, m],
            device_id=(s, to), device_id_type=MESH)

    def z_arrival(a, z):
        return pltpu.make_async_remote_copy(
            src_ref=srcs[a].at[:, columns(z)], dst_ref=kv.at[s * n_mlp + z, a],
            send_sem=z_send.at[a, z], recv_sem=z_recv.at[a, z],
            device_id=(s, z), device_id_type=MESH)

    def moved(src_p, src_c, z, to_s, send, recv):
        part = kv.at[(2 * src_p + src_c) * n_mlp + z]
        return pltpu.make_async_remote_copy(
            src_ref=part, dst_ref=part, send_sem=send, recv_sem=recv,
            device_id=(to_s, m), device_id_type=MESH)

    def own_copy(z, to_p):
        return moved(p, c, z, 2 * to_p + c, hop_send.at[z, to_p], hop_recv.at[z, p])

    def hop_arrival(z, src_p):
        return moved(src_p, c, z, 2 * src_p + c, hop_send.at[z, src_p], hop_recv.at[z, src_p])

    def own_sib_copy(z):
        return moved(p, c, z, sibling, own_sib_send.at[z], sib_recv.at[z, p])

    def sib_copy(z, src_p):
        return moved(src_p, c, z, sibling, sib_send.at[z, src_p], sib_recv.at[z, src_p])

    def sib_arrival(z, src_p):
        return moved(src_p, 1 - c, z, sibling, sib_send.at[z, src_p], sib_recv.at[z, src_p])

    def send_own(z):
        @pl.loop(p + 1, chips)
        def _(to_p):
            own_copy(z, to_p).start()

        @pl.when(c == 0)
        def _():
            own_sib_copy(z).start()

    def z_order(i):
        return lax.rem(m + i, n_mlp)

    def local_copy(a):
        return pltpu.make_async_copy(
            srcs[a].at[:, columns(m)], kv.at[s * n_mlp + m, a], local_sem.at[a])

    local_copy(0).start()
    local_copy(1).start()

    barrier = pltpu.get_barrier_semaphore()

    @pl.loop(1, n_mlp)
    def _(i):
        pl.semaphore_signal(barrier, inc=1, device_id=(s, z_order(i)), device_id_type=MESH)

    @pl.loop(1, chips)
    def _(i):
        pl.semaphore_signal(
            barrier, inc=1, device_id=(2 * lax.rem(p + i, chips) + c, m), device_id_type=MESH)

    pl.semaphore_signal(barrier, inc=1, device_id=(sibling, m), device_id_type=MESH)
    pl.semaphore_wait(barrier, n_mlp - 1 + chips - 1 + 1)

    @pl.loop(1, n_mlp)
    def _(i):
        z_copy(0, z_order(i)).start()
        z_copy(1, z_order(i)).start()

    local_copy(0).wait()
    local_copy(1).wait()
    send_own(m)

    listing = list_v[pl.ds(m * heads, heads)]
    own_list[...] = jnp.maximum(listing, 0)
    slots = lax.broadcasted_iota(jnp.int32, listing.shape, 2) + 1
    most = jnp.max(jnp.where(listing >= 0, slots, 0), axis=2, keepdims=True)
    used[...] = jnp.broadcast_to(jnp.max(most, axis=1, keepdims=True), used.shape)
    spread = (lax.broadcasted_iota(jnp.int32, (kmax, kmax * BLK), 1) // BLK
              == lax.broadcasted_iota(jnp.int32, (kmax, kmax * BLK), 0)).astype(jnp.bfloat16)
    inside = (lax.broadcasted_iota(jnp.int32, (q_blocks, kmax * BLK), 1) % BLK).astype(jnp.float32)

    @pl.loop(0, heads)
    def _(h):
        named = list_v[m * heads + h].astype(jnp.float32).astype(jnp.bfloat16)
        block = jnp.dot(named, spread, preferred_element_type=jnp.float32)
        kpos[h] = jnp.where(block < 0, FAR, block * BLK + inside)

    @pl.loop(1, n_mlp)
    def _(i):
        z = z_order(i)
        z_arrival(0, z).wait_recv()
        z_arrival(1, z).wait_recv()
        send_own(z)

    @pl.loop(0, n_mlp)
    def _(i):
        @pl.loop(0, p)
        def _(src_p):
            z = z_order(i)
            hop_arrival(z, src_p).wait_recv()
            sib_copy(z, src_p).start()

    @pl.loop(0, n_mlp)
    def _(z):
        @pl.loop(0, p + c)
        def _(src_p):
            sib_arrival(z, src_p).wait_recv()

    @pl.loop(1, n_mlp)
    def _(i):
        z_copy(0, z_order(i)).wait_send()
        z_copy(1, z_order(i)).wait_send()

    @pl.loop(0, n_mlp)
    def _(z):
        @pl.loop(p + 1, chips)
        def _(to_p):
            own_copy(z, to_p).wait_send()

        @pl.when(c == 0)
        def _():
            own_sib_copy(z).wait_send()

        @pl.loop(0, p)
        def _(src_p):
            sib_copy(z, src_p).wait_send()


def attend_kernel(
    own_list, used, kpos, q_hbm, kv_hbm, out_hbm, kbuf, vbuf, qbuf, out_buf, sem, out_sem,
):
    s = lax.axis_index("seq")
    m = lax.axis_index("mlp")
    heads, q_blocks, kmax = own_list.shape
    rows = q_blocks * BLK
    wide = heads * HD

    k_copy = pltpu.make_async_copy(kv_hbm.at[:, 0], kbuf, sem.at[0])
    v_copy = pltpu.make_async_copy(kv_hbm.at[:, 1], vbuf, sem.at[1])
    q_copy = pltpu.make_async_copy(
        q_hbm.at[:, pl.ds(pl.multiple_of(m * wide, wide), wide)], qbuf, sem.at[2])
    k_copy.start()
    q_copy.start()
    v_copy.start()

    factor = math.log2(math.e) / math.sqrt(HD)
    first = s * rows

    def lanes(index):
        return pl.ds(pl.multiple_of(index * HD, HD), HD)

    def out_copy(h):
        return pltpu.make_async_copy(out_buf.at[:, lanes(h)], out_hbm.at[:, lanes(h)], out_sem.at[h])

    def gathered(buf, h, qb, count):
        group = lanes(h // PER_GROUP)
        return jnp.concatenate([buf[own_list[h, qb, k], :, group] for k in range(count)], axis=0)

    def one_head(h, count):
        parts = [slice(qb * BLK, (qb + 1) * BLK) for qb in range(q_blocks)]
        scores = [
            lax.dot_general(
                qbuf[parts[qb], lanes(h)], gathered(kbuf, h, qb, count), (((1,), (1,)), ((), ())),
                preferred_element_type=jnp.float32)
            for qb in range(q_blocks)]
        positions = kpos[h, :, :count * BLK]
        weights, totals = [], []
        for qb in range(q_blocks):
            row = (lax.broadcasted_iota(jnp.int32, (BLK, 1), 0) + (first + qb * BLK)).astype(jnp.float32)
            masked = jnp.where(positions[qb:qb + 1, :] <= row, scores[qb], MASKED)
            top = jnp.max(masked, axis=1, keepdims=True)
            raised = jnp.exp2((masked - top) * factor)
            totals.append(jnp.sum(raised, axis=1, keepdims=True))
            weights.append(raised.astype(jnp.bfloat16))
        for qb in range(q_blocks):
            product = jnp.dot(weights[qb], gathered(vbuf, h, qb, count), preferred_element_type=jnp.float32)
            out_buf[parts[qb], lanes(h)] = (product / totals[qb]).astype(out_buf.dtype)

    k_copy.wait()
    q_copy.wait()
    v_copy.wait()
    steps = [kmax * i // 4 for i in range(1, 5)]

    @pl.loop(0, heads)
    def _(h):
        need = used[h, 0, 0]
        for low, high in zip([0] + steps, steps):
            @pl.when(jnp.logical_and(need > low, need <= high))
            def _():
                one_head(h, high)

        out_copy(h).start()

    @pl.loop(0, heads)
    def _(h):
        out_copy(h).wait()


def body(n_seq, n_mlp, query_rows, key_rows, value_rows, key_blocks):
    piece = key_rows.shape[0]
    rows = query_rows.shape[0]
    heads = H // n_mlp
    width = (KVH // n_mlp) * HD
    q_blocks, kmax = key_blocks.shape[1:]
    chips = n_seq // 2
    blocks = n_seq * n_mlp
    dma = pltpu.SemaphoreType.DMA
    whole = pl.BlockSpec(memory_space=pltpu.VMEM)
    anywhere = pl.BlockSpec(memory_space=pl.ANY)
    scalars = pl.BlockSpec(memory_space=pltpu.SMEM)
    kv, kpos, own_list, used = pl.pallas_call(
        functools.partial(gather_kernel, n_seq, n_mlp),
        out_shape=(
            jax.ShapeDtypeStruct((blocks, 2, piece, width), jnp.bfloat16),
            jax.ShapeDtypeStruct((heads, q_blocks, kmax * BLK), jnp.float32),
            jax.ShapeDtypeStruct((heads, q_blocks, kmax), jnp.int32),
            jax.ShapeDtypeStruct((heads, 1, 128), jnp.int32),
        ),
        in_specs=[whole, anywhere, anywhere],
        out_specs=(anywhere, whole, whole, whole),
        scratch_shapes=[
            dma((2,)),
            dma((2, n_mlp)),
            dma((2, n_mlp)),
            dma((n_mlp, chips)),
            dma((n_mlp, chips)),
            dma((n_mlp,)),
            dma((n_mlp, chips)),
            dma((n_mlp, chips)),
        ],
        compiler_params=pltpu.CompilerParams(collective_id=0, has_side_effects=True),
        name="gather_keys_values",
    )(key_blocks, key_rows, value_rows)
    return pl.pallas_call(
        attend_kernel,
        out_shape=jax.ShapeDtypeStruct((rows, heads * HD), jnp.bfloat16),
        in_specs=[scalars, scalars, whole, anywhere, anywhere],
        out_specs=anywhere,
        scratch_shapes=[
            pltpu.VMEM((blocks, piece, width), jnp.bfloat16),
            pltpu.VMEM((blocks, piece, width), jnp.bfloat16),
            pltpu.VMEM((rows, heads * HD), jnp.bfloat16),
            pltpu.VMEM((rows, heads * HD), jnp.bfloat16),
            dma((3,)),
            dma((heads,)),
        ],
        compiler_params=pltpu.CompilerParams(vmem_limit_bytes=48 * 1024 * 1024),
        name="attend_listed_blocks",
    )(own_list, used, kpos, query_rows, kv)


def solution(mesh):
    placed = (
        P("seq", None),
        P(("seq", "mlp"), None),
        P(("seq", "mlp"), None),
        P(None, "seq", None),
    )
    return jax.shard_map(
        functools.partial(body, mesh.shape["seq"], mesh.shape["mlp"]),
        mesh=mesh, in_specs=placed, out_specs=P("seq", "mlp"), check_vma=False
    )
```

```python
import functools
import math

import jax
import jax.numpy as jnp
from jax import lax
from jax.experimental import pallas as pl
from jax.experimental.pallas import tpu as pltpu
from jax.sharding import PartitionSpec as P

H = 64
KVH = 8
HD = 128
BLK = 64
PER_GROUP = H // KVH

MESH = pl.DeviceIdType.MESH
MASKED = -1e30


def gather_kernel(
    n_seq, n_mlp, list_v, k_hbm, v_hbm, kv, used,
    local_sem, z_send, z_recv, hop_send, hop_recv, own_sib_send, sib_send, sib_recv,
):
    s = lax.axis_index("seq")
    m = lax.axis_index("mlp")
    chips = n_seq // 2
    p, c = s // 2, s % 2
    width = kv.shape[3]
    srcs = (k_hbm, v_hbm)
    sibling = 2 * p + 1 - c

    def columns(z):
        return pl.ds(pl.multiple_of(z * width, width), width)

    def z_copy(a, to):
        return pltpu.make_async_remote_copy(
            src_ref=srcs[a].at[:, columns(to)], dst_ref=kv.at[s * n_mlp + m, a],
            send_sem=z_send.at[a, to], recv_sem=z_recv.at[a, m],
            device_id=(s, to), device_id_type=MESH)

    def z_arrival(a, z):
        return pltpu.make_async_remote_copy(
            src_ref=srcs[a].at[:, columns(z)], dst_ref=kv.at[s * n_mlp + z, a],
            send_sem=z_send.at[a, z], recv_sem=z_recv.at[a, z],
            device_id=(s, z), device_id_type=MESH)

    def moved(src_p, src_c, z, to_s, send, recv):
        part = kv.at[(2 * src_p + src_c) * n_mlp + z]
        return pltpu.make_async_remote_copy(
            src_ref=part, dst_ref=part, send_sem=send, recv_sem=recv,
            device_id=(to_s, m), device_id_type=MESH)

    def own_copy(z, to_p):
        return moved(p, c, z, 2 * to_p + c, hop_send.at[z, to_p], hop_recv.at[z, p])

    def hop_arrival(z, src_p):
        return moved(src_p, c, z, 2 * src_p + c, hop_send.at[z, src_p], hop_recv.at[z, src_p])

    def own_sib_copy(z):
        return moved(p, c, z, sibling, own_sib_send.at[z], sib_recv.at[z, p])

    def sib_copy(z, src_p):
        return moved(src_p, c, z, sibling, sib_send.at[z, src_p], sib_recv.at[z, src_p])

    def sib_arrival(z, src_p):
        return moved(src_p, 1 - c, z, sibling, sib_send.at[z, src_p], sib_recv.at[z, src_p])

    def send_own(z):
        @pl.loop(p + 1, chips)
        def _(to_p):
            own_copy(z, to_p).start()

        @pl.when(c == 0)
        def _():
            own_sib_copy(z).start()

    def z_order(i):
        return lax.rem(m + i, n_mlp)

    def local_copy(a):
        return pltpu.make_async_copy(
            srcs[a].at[:, columns(m)], kv.at[s * n_mlp + m, a], local_sem.at[a])

    local_copy(0).start()
    local_copy(1).start()

    barrier = pltpu.get_barrier_semaphore()

    @pl.loop(1, n_mlp)
    def _(i):
        pl.semaphore_signal(barrier, inc=1, device_id=(s, z_order(i)), device_id_type=MESH)

    @pl.loop(1, chips)
    def _(i):
        pl.semaphore_signal(
            barrier, inc=1, device_id=(2 * lax.rem(p + i, chips) + c, m), device_id_type=MESH)

    pl.semaphore_signal(barrier, inc=1, device_id=(sibling, m), device_id_type=MESH)
    pl.semaphore_wait(barrier, n_mlp - 1 + chips - 1 + 1)

    @pl.loop(1, n_mlp)
    def _(i):
        z_copy(0, z_order(i)).start()
        z_copy(1, z_order(i)).start()

    local_copy(0).wait()
    local_copy(1).wait()
    send_own(m)

    slots = lax.broadcasted_iota(jnp.int32, list_v.shape, 1) + 1
    most = jnp.max(jnp.where(list_v[...] >= 0, slots, 0), axis=1)
    used[...] = jnp.broadcast_to(jnp.max(most, axis=0, keepdims=True), used.shape)

    @pl.loop(1, n_mlp)
    def _(i):
        z = z_order(i)
        z_arrival(0, z).wait_recv()
        z_arrival(1, z).wait_recv()
        send_own(z)

    @pl.loop(0, n_mlp)
    def _(i):
        @pl.loop(0, p)
        def _(src_p):
            z = z_order(i)
            hop_arrival(z, src_p).wait_recv()
            sib_copy(z, src_p).start()

    @pl.loop(0, n_mlp)
    def _(z):
        @pl.loop(0, p + c)
        def _(src_p):
            sib_arrival(z, src_p).wait_recv()

    @pl.loop(1, n_mlp)
    def _(i):
        z_copy(0, z_order(i)).wait_send()
        z_copy(1, z_order(i)).wait_send()

    @pl.loop(0, n_mlp)
    def _(z):
        @pl.loop(p + 1, chips)
        def _(to_p):
            own_copy(z, to_p).wait_send()

        @pl.when(c == 0)
        def _():
            own_sib_copy(z).wait_send()

        @pl.loop(0, p)
        def _(src_p):
            sib_copy(z, src_p).wait_send()


def attend_kernel(
    list_hbm, used_hbm, kv_hbm, q_hbm, out_hbm, listing, used, kbuf, vbuf, vt_low, vt_high, qbuf, out_buf,
    sem, out_sem,
):
    s = lax.axis_index("seq")
    m = lax.axis_index("mlp")
    q_blocks, kmax = listing.shape[:2]
    wide = out_buf.shape[1]
    heads = wide // HD
    groups = heads // PER_GROUP
    pair_rows = 2 * BLK

    v_copy = pltpu.make_async_copy(kv_hbm.at[:, 1], vbuf, sem.at[3])
    v_copy.start()
    copies = [
        pltpu.make_async_copy(kv_hbm.at[:, 0], kbuf, sem.at[4]),
        pltpu.make_async_copy(
            q_hbm.at[:, pl.ds(pl.multiple_of(m * wide, wide), wide)], qbuf, sem.at[0]),
        pltpu.make_async_copy(list_hbm, listing, sem.at[1]),
        pltpu.make_async_copy(used_hbm, used, sem.at[2]),
    ]
    for copy in copies:
        copy.start()

    factor = math.log2(math.e) / math.sqrt(HD)
    lane = lax.broadcasted_iota(jnp.int32, (1, pair_rows), 1)
    low = lane < BLK
    lane_row = lax.rem(lane, BLK)
    low_rows = lax.broadcasted_iota(jnp.int32, (pair_rows, HD), 0) < BLK
    key_row = lax.broadcasted_iota(jnp.int32, (BLK, pair_rows), 0)

    def lanes(index):
        return pl.ds(pl.multiple_of(index * HD, HD), HD)

    v_copy.wait()

    @pl.loop(0, (s + 1) * (q_blocks // 2))
    def _(i):
        for group in range(groups):
            part = slice(group * HD, (group + 1) * HD)
            even = vbuf[2 * i, :, part].astype(jnp.float32)
            odd = vbuf[2 * i + 1, :, part].astype(jnp.float32)
            ahead = jnp.concatenate([even, odd], axis=0).T
            behind = jnp.concatenate([odd, even], axis=0).T
            vt_low[group, 2 * i] = jnp.where(low, ahead, 0.0).astype(jnp.bfloat16)
            vt_low[group, 2 * i + 1] = jnp.where(low, behind, 0.0).astype(jnp.bfloat16)
            vt_high[group, 2 * i] = jnp.where(low, 0.0, behind).astype(jnp.bfloat16)
            vt_high[group, 2 * i + 1] = jnp.where(low, 0.0, ahead).astype(jnp.bfloat16)

    for copy in copies:
        copy.wait()

    def out_copy(h):
        return pltpu.make_async_copy(out_buf.at[:, lanes(h)], out_hbm.at[:, lanes(h)], out_sem.at[h])

    def one_head(h, count):
        group = h // PER_GROUP
        pairs = range(q_blocks // 2)
        names = [[listing[qb, k, m * heads + h] for k in range(count)] for qb in range(q_blocks)]
        places = [[jnp.maximum(name, 0) for name in row] for row in names]
        scores = []
        for pair in pairs:
            queries = qbuf[pair * pair_rows:(pair + 1) * pair_rows, lanes(h)]
            zero = jnp.zeros_like(queries)
            split = jnp.concatenate(
                [jnp.where(low_rows, queries, zero), jnp.where(low_rows, zero, queries)], axis=1)
            keys = jnp.concatenate(
                [jnp.concatenate([kbuf[b, :, lanes(group)] for b in places[2 * pair + j]], axis=0)
                 for j in range(2)], axis=1)
            scores.append(lax.dot_general(
                keys, split, (((1,), (1,)), ((), ())), preferred_element_type=jnp.float32))
        weights, totals = [], []
        for pair in pairs:
            masked = []
            for k in range(count):
                reach = []
                for j in range(2):
                    qb = 2 * pair + j
                    name = names[qb][k]
                    reach.append(jnp.where(name < 0, -BLK, (s * q_blocks + qb - name) * BLK))
                limit = jnp.where(low, reach[0], reach[1]) + lane_row
                part = scores[pair][k * BLK:(k + 1) * BLK]
                masked.append(jnp.where(key_row <= limit, part, MASKED))
            masked = jnp.concatenate(masked, axis=0)
            top = jnp.max(masked, axis=0, keepdims=True)
            raised = jnp.exp2((masked - top) * factor)
            totals.append(jnp.sum(raised, axis=0, keepdims=True))
            weights.append(raised.astype(jnp.bfloat16))
        for pair in pairs:
            values = jnp.concatenate(
                [jnp.concatenate(
                    [vt_low[group, places[2 * pair + j][k]] + vt_high[group, places[2 * pair + j][k + 1]]
                     for k in range(0, count, 2)], axis=1)
                 for j in range(2)], axis=0)
            product = jnp.dot(values, weights[pair], preferred_element_type=jnp.float32)
            both = jnp.where(low, product[:HD], product[HD:]) / totals[pair]
            out_buf[pair * pair_rows:(pair + 1) * pair_rows, lanes(h)] = both.T.astype(out_buf.dtype)

    steps = [kmax * i // 4 for i in range(1, 5)]

    @pl.loop(0, heads)
    def _(h):
        need = used[0, m * heads + h]
        for below, high in zip([0] + steps, steps):
            @pl.when(jnp.logical_and(need > below, need <= high))
            def _():
                one_head(h, high)

        out_copy(h).start()

    @pl.loop(0, heads)
    def _(h):
        out_copy(h).wait()


def body(n_seq, n_mlp, query_rows, key_rows, value_rows, key_blocks):
    piece = key_rows.shape[0]
    rows = query_rows.shape[0]
    heads = H // n_mlp
    width = (KVH // n_mlp) * HD
    q_blocks, kmax = key_blocks.shape[1:]
    chips = n_seq // 2
    blocks = n_seq * n_mlp
    listing = jnp.transpose(key_blocks, (1, 2, 0))
    dma = pltpu.SemaphoreType.DMA
    whole = pl.BlockSpec(memory_space=pltpu.VMEM)
    anywhere = pl.BlockSpec(memory_space=pl.ANY)
    kv, used = pl.pallas_call(
        functools.partial(gather_kernel, n_seq, n_mlp),
        out_shape=(
            jax.ShapeDtypeStruct((blocks, 2, piece, width), jnp.bfloat16),
            jax.ShapeDtypeStruct((8, H), jnp.int32),
        ),
        in_specs=[whole, anywhere, anywhere],
        out_specs=(anywhere, whole),
        scratch_shapes=[
            dma((2,)),
            dma((2, n_mlp)),
            dma((2, n_mlp)),
            dma((n_mlp, chips)),
            dma((n_mlp, chips)),
            dma((n_mlp,)),
            dma((n_mlp, chips)),
            dma((n_mlp, chips)),
        ],
        compiler_params=pltpu.CompilerParams(collective_id=0, has_side_effects=True, vmem_limit_bytes=62 * 1024 * 1024),
        name="gather_keys_values",
    )(listing, key_rows, value_rows)
    return pl.pallas_call(
        attend_kernel,
        out_shape=jax.ShapeDtypeStruct((rows, heads * HD), jnp.bfloat16),
        in_specs=[anywhere] * 4,
        out_specs=anywhere,
        scratch_shapes=[
            pltpu.SMEM((q_blocks, kmax, H), jnp.int32),
            pltpu.SMEM((8, H), jnp.int32),
            pltpu.VMEM((blocks, piece, width), jnp.bfloat16),
            pltpu.VMEM((blocks, piece, width), jnp.bfloat16),
            pltpu.VMEM((width // HD, blocks, HD, 2 * BLK), jnp.bfloat16),
            pltpu.VMEM((width // HD, blocks, HD, 2 * BLK), jnp.bfloat16),
            pltpu.VMEM((rows, heads * HD), jnp.bfloat16),
            pltpu.VMEM((rows, heads * HD), jnp.bfloat16),
            dma((5,)),
            dma((heads,)),
        ],
        compiler_params=pltpu.CompilerParams(vmem_limit_bytes=62 * 1024 * 1024),
        name="attend_listed_blocks",
    )(listing, used, kv, query_rows)


def solution(mesh):
    placed = (
        P("seq", None),
        P(("seq", "mlp"), None),
        P(("seq", "mlp"), None),
        P(None, "seq", None),
    )
    return jax.shard_map(
        functools.partial(body, mesh.shape["seq"], mesh.shape["mlp"]),
        mesh=mesh, in_specs=placed, out_specs=P("seq", "mlp"), check_vma=False
    )
```

```python
import functools
import math

import jax
import jax.numpy as jnp
from jax import lax
from jax.experimental import pallas as pl
from jax.experimental.pallas import tpu as pltpu
from jax.sharding import PartitionSpec as P

H = 64
KVH = 8
HD = 128
BLK = 64
PER_GROUP = H // KVH

MESH = pl.DeviceIdType.MESH
MASKED = -1e30
FAR = 1e9


def gather_kernel(
    n_seq, n_mlp, list_v, k_hbm, v_hbm, kv, kpos, plan, spaced,
    local_sem, z_send, z_recv, hop_send, hop_recv, relay_send, own_sib_send, sib_send, sib_recv,
):
    s = lax.axis_index("seq")
    m = lax.axis_index("mlp")
    chips = n_seq // 2
    p, c = s // 2, s % 2
    width = kv.shape[3]
    q_blocks, kmax = list_v.shape[:2]
    heads = H // n_mlp
    srcs = (k_hbm, v_hbm)
    sibling = 2 * p + 1 - c

    def columns(z):
        return pl.ds(pl.multiple_of(z * width, width), width)

    def z_copy(a, to):
        return pltpu.make_async_remote_copy(
            src_ref=srcs[a].at[:, columns(to)], dst_ref=kv.at[s * n_mlp + m, a],
            send_sem=z_send.at[a, to], recv_sem=z_recv.at[a, m],
            device_id=(s, to), device_id_type=MESH)

    def z_arrival(a, z):
        return pltpu.make_async_remote_copy(
            src_ref=srcs[a].at[:, columns(z)], dst_ref=kv.at[s * n_mlp + z, a],
            send_sem=z_send.at[a, z], recv_sem=z_recv.at[a, z],
            device_id=(s, z), device_id_type=MESH)

    def moved(src_p, src_c, z, to_s, send, recv):
        part = kv.at[(2 * src_p + src_c) * n_mlp + z]
        return pltpu.make_async_remote_copy(
            src_ref=part, dst_ref=part, send_sem=send, recv_sem=recv,
            device_id=(to_s, m), device_id_type=MESH)

    def own_copy(z, to_p):
        return moved(p, c, z, 2 * to_p + c, hop_send.at[z, to_p], hop_recv.at[z, p])

    def hop_arrival(z, src_p):
        return moved(src_p, c, z, 2 * src_p + c, hop_send.at[z, src_p], hop_recv.at[z, src_p])

    def own_sib_copy(z):
        return moved(p, c, z, sibling, own_sib_send.at[z], sib_recv.at[z, p])

    def sib_copy(z, src_p):
        return moved(src_p, c, z, sibling, sib_send.at[z, src_p], sib_recv.at[z, src_p])

    def sib_arrival(z, src_p):
        return moved(src_p, 1 - c, z, sibling, sib_send.at[z, src_p], sib_recv.at[z, src_p])

    def relay_copy(z, src_p, to_p):
        return moved(src_p, c, z, 2 * to_p + c, relay_send.at[z], hop_recv.at[z, src_p])

    small = chips == 4
    passes_zero = jnp.logical_and(small, p == 1 + c)
    passes_one = jnp.logical_and(small, p == 3 * c)

    def each_target(act):
        @pl.loop(0, chips)
        def _(to_p):
            wanted = to_p > p
            if small:
                wanted = jnp.logical_and(wanted, p + to_p != 3)
                wanted = jnp.logical_or(wanted, jnp.logical_and(p == 1, jnp.logical_and(c == 0, to_p == 0)))
            @pl.when(wanted)
            def _():
                act(to_p)

    def each_relay(z, src_p, act):
        if small:
            @pl.when(jnp.logical_and(passes_zero, src_p == 0))
            def _():
                act(relay_copy(z, 0, 3))

            @pl.when(jnp.logical_and(passes_one, src_p == 1))
            def _():
                act(relay_copy(z, 1, 2))

    def send_own(z):
        each_target(lambda to_p: own_copy(z, to_p).start())

        @pl.when(c == 0)
        def _():
            own_sib_copy(z).start()

    def z_order(i):
        return lax.rem(m + i, n_mlp)

    def local_copy(a):
        return pltpu.make_async_copy(
            srcs[a].at[:, columns(m)], kv.at[s * n_mlp + m, a], local_sem.at[a])

    local_copy(0).start()
    local_copy(1).start()

    barrier = pltpu.get_barrier_semaphore()

    @pl.loop(1, n_mlp)
    def _(i):
        pl.semaphore_signal(barrier, inc=1, device_id=(s, z_order(i)), device_id_type=MESH)

    @pl.loop(1, chips)
    def _(i):
        pl.semaphore_signal(
            barrier, inc=1, device_id=(2 * lax.rem(p + i, chips) + c, m), device_id_type=MESH)

    pl.semaphore_signal(barrier, inc=1, device_id=(sibling, m), device_id_type=MESH)
    pl.semaphore_wait(barrier, n_mlp - 1 + chips - 1 + 1)

    @pl.loop(1, n_mlp)
    def _(i):
        z_copy(0, z_order(i)).start()
        z_copy(1, z_order(i)).start()

    local_copy(0).wait()
    local_copy(1).wait()
    send_own(m)

    slots = lax.broadcasted_iota(jnp.int32, list_v.shape, 1) + 1
    most = jnp.max(jnp.where(list_v[...] >= 0, slots, 0), axis=1)
    used = jnp.max(most, axis=0, keepdims=True).astype(jnp.float32)
    across = lax.broadcasted_iota(jnp.int32, (H, H), 1)
    down = lax.broadcasted_iota(jnp.int32, (H, H), 0)
    other = jnp.broadcast_to(used, (H, H))
    mine = jnp.sum(jnp.where(across == down, other, 0.0), axis=1, keepdims=True)
    ahead = jnp.logical_or(other > mine, jnp.logical_and(other == mine, across < down))
    ahead = jnp.logical_and(ahead, across // heads == down // heads)
    rank = jnp.sum(jnp.where(ahead, 1.0, 0.0), axis=1, keepdims=True)
    holds = jnp.logical_and(rank == across.astype(jnp.float32), down // heads == m)
    order = jnp.sum(jnp.where(holds, (down - m * heads).astype(jnp.float32), 0.0), axis=0, keepdims=True)
    plan_row = lax.broadcasted_iota(jnp.int32, plan.shape, 0)
    plan[...] = jnp.where(plan_row == 0, used, order).astype(jnp.int32)

    spread = (lax.broadcasted_iota(jnp.int32, (kmax, kmax * BLK), 1) // BLK
              == lax.broadcasted_iota(jnp.int32, (kmax, kmax * BLK), 0)).astype(jnp.bfloat16)
    inside = (lax.broadcasted_iota(jnp.int32, (heads, kmax * BLK), 1) % BLK).astype(jnp.float32)
    for qb in range(q_blocks):
        named = list_v[qb].astype(jnp.float32).astype(jnp.bfloat16)
        spaced[...] = lax.dot_general(
            named, spread, (((0,), (0,)), ((), ())), preferred_element_type=jnp.float32)
        block = spaced[pl.ds(pl.multiple_of(m * heads, heads), heads), :]
        kpos[qb] = jnp.where(block < 0, FAR, block * BLK + inside)

    @pl.loop(1, n_mlp)
    def _(i):
        z = z_order(i)
        z_arrival(0, z).wait_recv()
        z_arrival(1, z).wait_recv()
        send_own(z)

    @pl.loop(0, n_mlp)
    def _(i):
        z = z_order(i)

        @pl.loop(0, p)
        def _(j):
            src_p = jnp.where(p == 3, lax.rem(j + 1, 3), j) if small else j
            hop_arrival(z, src_p).wait_recv()
            each_relay(z, src_p, lambda copy: copy.start())
            sib_copy(z, src_p).start()

        if small:
            @pl.when(jnp.logical_and(p == 0, c == 0))
            def _():
                hop_arrival(z, 1).wait_recv()
                each_relay(z, 1, lambda copy: copy.start())

    @pl.loop(0, n_mlp)
    def _(z):
        @pl.loop(0, p + c)
        def _(src_p):
            sib_arrival(z, src_p).wait_recv()

    @pl.loop(1, n_mlp)
    def _(i):
        z_copy(0, z_order(i)).wait_send()
        z_copy(1, z_order(i)).wait_send()

    @pl.loop(0, n_mlp)
    def _(z):
        each_target(lambda to_p: own_copy(z, to_p).wait_send())
        for src_p in range(2):
            each_relay(z, src_p, lambda copy: copy.wait_send())

        @pl.when(c == 0)
        def _():
            own_sib_copy(z).wait_send()

        @pl.loop(0, p)
        def _(src_p):
            sib_copy(z, src_p).wait_send()


def attend_kernel(
    list_hbm, plan_hbm, kpos, kv_hbm, q_hbm, out_hbm, listing, plan, kbuf, vbuf, qbuf, out_buf,
    sem, out_sem,
):
    s = lax.axis_index("seq")
    m = lax.axis_index("mlp")
    q_blocks, kmax = listing.shape[:2]
    wide = out_buf.shape[1]
    heads = wide // HD
    rows = q_blocks * BLK
    together = 4 if kmax <= 16 else 1

    copies = [
        pltpu.make_async_copy(plan_hbm, plan, sem.at[0]),
        pltpu.make_async_copy(list_hbm, listing, sem.at[1]),
        pltpu.make_async_copy(
            q_hbm.at[:, pl.ds(pl.multiple_of(m * wide, wide), wide)], qbuf, sem.at[2]),
        pltpu.make_async_copy(kv_hbm.at[:, 0], kbuf, sem.at[3]),
        pltpu.make_async_copy(kv_hbm.at[:, 1], vbuf, sem.at[4]),
    ]
    for copy in copies:
        copy.start()

    factor = math.log2(math.e) / math.sqrt(HD)
    first = s * rows
    parts = [slice(qb * BLK, (qb + 1) * BLK) for qb in range(q_blocks)]
    row_in_block = lax.broadcasted_iota(jnp.int32, (BLK, 1), 0)

    def lanes(index):
        return pl.ds(pl.multiple_of(index * HD, HD), HD)

    def out_copy(h):
        return pltpu.make_async_copy(out_buf.at[:, lanes(h)], out_hbm.at[:, lanes(h)], out_sem.at[h])

    def attend(members, count):
        places = [
            [[jnp.maximum(listing[qb, k, m * heads + h], 0) for k in range(count)]
             for qb in range(q_blocks)] for h in members]
        scores, weights, totals = {}, {}, {}

        def gathered(buf, j, qb):
            group = lanes(members[j] // PER_GROUP)
            return jnp.concatenate([buf[b, :, group] for b in places[j][qb]], axis=0)

        def score(j):
            for qb in range(q_blocks):
                scores[j, qb] = lax.dot_general(
                    qbuf[parts[qb], lanes(members[j])], gathered(kbuf, j, qb), (((1,), (1,)), ((), ())),
                    preferred_element_type=jnp.float32)

        def weigh(j):
            for qb in range(q_blocks):
                row = (row_in_block + (first + qb * BLK)).astype(jnp.float32)
                position = kpos[qb, pl.ds(members[j], 1), :count * BLK]
                masked = jnp.where(position <= row, scores.pop((j, qb)), MASKED)
                top = jnp.max(masked, axis=1, keepdims=True)
                raised = jnp.exp2((masked - top) * factor)
                totals[j, qb] = jnp.sum(raised, axis=1, keepdims=True)
                weights[j, qb] = raised.astype(jnp.bfloat16)

        def combine(j):
            for qb in range(q_blocks):
                product = jnp.dot(
                    weights.pop((j, qb)), gathered(vbuf, j, qb), preferred_element_type=jnp.float32)
                out_buf[parts[qb], lanes(members[j])] = (product / totals.pop((j, qb))).astype(out_buf.dtype)

        for step in range(len(members) + 2):
            for stage, lag in ((combine, 2), (weigh, 1), (score, 0)):
                if 0 <= step - lag < len(members):
                    stage(step - lag)

    for copy in copies:
        copy.wait()
    steps = [kmax * i // 4 for i in range(1, 5)]

    @pl.loop(0, heads // together)
    def _(t):
        members = [plan[1, t * together + j] for j in range(together)]
        need = plan[0, m * heads + members[0]]
        for below, high in zip([0] + steps, steps):
            @pl.when(jnp.logical_and(need > below, need <= high))
            def _():
                attend(members, high)

        for h in members:
            out_copy(h).start()

    @pl.loop(0, heads)
    def _(h):
        out_copy(h).wait()


def body(n_seq, n_mlp, query_rows, key_rows, value_rows, key_blocks):
    piece = key_rows.shape[0]
    rows = query_rows.shape[0]
    heads = H // n_mlp
    width = (KVH // n_mlp) * HD
    q_blocks, kmax = key_blocks.shape[1:]
    chips = n_seq // 2
    blocks = n_seq * n_mlp
    listing = jnp.transpose(key_blocks, (1, 2, 0))
    dma = pltpu.SemaphoreType.DMA
    whole = pl.BlockSpec(memory_space=pltpu.VMEM)
    anywhere = pl.BlockSpec(memory_space=pl.ANY)
    kv, kpos, plan = pl.pallas_call(
        functools.partial(gather_kernel, n_seq, n_mlp),
        out_shape=(
            jax.ShapeDtypeStruct((blocks, 2, piece, width), jnp.bfloat16),
            jax.ShapeDtypeStruct((q_blocks, heads, kmax * BLK), jnp.float32),
            jax.ShapeDtypeStruct((8, H), jnp.int32),
        ),
        in_specs=[whole, anywhere, anywhere],
        out_specs=(anywhere, whole, whole),
        scratch_shapes=[
            pltpu.VMEM((H, kmax * BLK), jnp.float32),
            dma((2,)),
            dma((2, n_mlp)),
            dma((2, n_mlp)),
            dma((n_mlp, chips)),
            dma((n_mlp, chips)),
            dma((n_mlp,)),
            dma((n_mlp,)),
            dma((n_mlp, chips)),
            dma((n_mlp, chips)),
        ],
        compiler_params=pltpu.CompilerParams(collective_id=0, has_side_effects=True, vmem_limit_bytes=62 * 1024 * 1024),
        name="gather_keys_values",
    )(listing, key_rows, value_rows)
    return pl.pallas_call(
        attend_kernel,
        out_shape=jax.ShapeDtypeStruct((rows, heads * HD), jnp.bfloat16),
        in_specs=[anywhere, anywhere, whole, anywhere, anywhere],
        out_specs=anywhere,
        scratch_shapes=[
            pltpu.SMEM((q_blocks, kmax, H), jnp.int32),
            pltpu.SMEM((8, H), jnp.int32),
            pltpu.VMEM((blocks, piece, width), jnp.bfloat16),
            pltpu.VMEM((blocks, piece, width), jnp.bfloat16),
            pltpu.VMEM((rows, heads * HD), jnp.bfloat16),
            pltpu.VMEM((rows, heads * HD), jnp.bfloat16),
            dma((5,)),
            dma((heads,)),
        ],
        compiler_params=pltpu.CompilerParams(vmem_limit_bytes=62 * 1024 * 1024),
        name="attend_listed_blocks",
    )(listing, plan, kpos, kv, query_rows)


def solution(mesh):
    placed = (
        P("seq", None),
        P(("seq", "mlp"), None),
        P(("seq", "mlp"), None),
        P(None, "seq", None),
    )
    return jax.shard_map(
        functools.partial(body, mesh.shape["seq"], mesh.shape["mlp"]),
        mesh=mesh, in_specs=placed, out_specs=P("seq", "mlp"), check_vma=False
    )
```

```python
import functools
import math

import jax
import jax.numpy as jnp
from jax import lax
from jax.experimental import pallas as pl
from jax.experimental.pallas import tpu as pltpu
from jax.sharding import PartitionSpec as P

H = 64
KVH = 8
HD = 128
BLK = 64
PER_GROUP = H // KVH

MESH = pl.DeviceIdType.MESH
MASKED = -1e30
FAR = 1e9


def lanes(index, size=HD):
    return pl.ds(pl.multiple_of(index * size, size), size)


def score_kernel(
    n_seq, n_mlp, list_s, list_v, q_hbm, k_hbm, v_hbm, v_out, p_out, plan,
    kbuf, qbuf, kpos, spaced, probs,
    local_sem, p_sem, z_send, z_recv, hop_send, hop_recv, own_sib_send, sib_send, sib_recv,
):
    s = lax.axis_index("seq")
    m = lax.axis_index("mlp")
    chips = n_seq // 2
    p, c = s // 2, s % 2
    width = kbuf.shape[2]
    q_blocks, kmax = list_v.shape[:2]
    heads = H // n_mlp
    together = 4 if kmax <= 16 else 1
    srcs = (k_hbm, v_hbm)
    bufs = (kbuf, v_out)
    sibling = 2 * p + 1 - c

    def z_copy(a, to):
        return pltpu.make_async_remote_copy(
            src_ref=srcs[a].at[:, lanes(to, width)], dst_ref=bufs[a].at[s * n_mlp + m],
            send_sem=z_send.at[a, to], recv_sem=z_recv.at[a, m],
            device_id=(s, to), device_id_type=MESH)

    def z_arrival(a, z):
        return pltpu.make_async_remote_copy(
            src_ref=srcs[a].at[:, lanes(z, width)], dst_ref=bufs[a].at[s * n_mlp + z],
            send_sem=z_send.at[a, z], recv_sem=z_recv.at[a, z],
            device_id=(s, z), device_id_type=MESH)

    def moved(a, src_p, src_c, z, to_s, send, recv):
        part = bufs[a].at[(2 * src_p + src_c) * n_mlp + z]
        return pltpu.make_async_remote_copy(
            src_ref=part, dst_ref=part, send_sem=send, recv_sem=recv,
            device_id=(to_s, m), device_id_type=MESH)

    def own_copy(a, z, to_p):
        return moved(a, p, c, z, 2 * to_p + c, hop_send.at[a, z, to_p], hop_recv.at[a, z, p])

    def hop_arrival(a, z, src_p):
        return moved(a, src_p, c, z, 2 * src_p + c, hop_send.at[a, z, src_p], hop_recv.at[a, z, src_p])

    def own_sib_copy(a, z):
        return moved(a, p, c, z, sibling, own_sib_send.at[a, z], sib_recv.at[a, z, p])

    def sib_copy(a, z, src_p):
        return moved(a, src_p, c, z, sibling, sib_send.at[a, z, src_p], sib_recv.at[a, z, src_p])

    def sib_arrival(a, z, src_p):
        return moved(a, src_p, 1 - c, z, sibling, sib_send.at[a, z, src_p], sib_recv.at[a, z, src_p])

    def send_own(a, z):
        @pl.loop(p + 1, chips)
        def _(to_p):
            own_copy(a, z, to_p).start()

        @pl.when(c == 0)
        def _():
            own_sib_copy(a, z).start()

    def pass_on(a, z):
        @pl.loop(0, p)
        def _(src_p):
            hop_arrival(a, z, src_p).wait_recv()
            sib_copy(a, z, src_p).start()

    def finish(a):
        @pl.loop(0, n_mlp)
        def _(z):
            @pl.loop(0, p + c)
            def _(src_p):
                sib_arrival(a, z, src_p).wait_recv()

    def z_order(i):
        if n_mlp != 4:
            return lax.rem(m + i, n_mlp)
        second = jnp.where(jnp.logical_or(m == 0, m == 2), 1, 2)
        third = jnp.where(m == 0, 2, jnp.where(m == 1, 0, jnp.where(m == 2, 3, 1)))
        last = jnp.where(m < 2, 3, 0)
        return jnp.where(i == 0, m, jnp.where(i == 1, second, jnp.where(i == 2, third, last)))

    def local_copy(a):
        return pltpu.make_async_copy(
            srcs[a].at[:, lanes(m, width)], bufs[a].at[s * n_mlp + m], local_sem.at[a])

    q_copy = pltpu.make_async_copy(q_hbm.at[:, lanes(m, heads * HD)], qbuf, local_sem.at[2])
    local_copy(0).start()
    local_copy(1).start()

    barrier = pltpu.get_barrier_semaphore()

    @pl.loop(1, n_mlp)
    def _(i):
        pl.semaphore_signal(barrier, inc=1, device_id=(s, z_order(i)), device_id_type=MESH)

    @pl.loop(1, chips)
    def _(i):
        pl.semaphore_signal(
            barrier, inc=1, device_id=(2 * lax.rem(p + i, chips) + c, m), device_id_type=MESH)

    pl.semaphore_signal(barrier, inc=1, device_id=(sibling, m), device_id_type=MESH)
    pl.semaphore_wait(barrier, n_mlp - 1 + chips - 1 + 1)

    for a in range(2):
        @pl.loop(1, n_mlp)
        def _(i):
            z_copy(a, z_order(i)).start()

    q_copy.start()
    for a in range(2):
        local_copy(a).wait()
        send_own(a, m)

        @pl.loop(1, n_mlp)
        def _(i):
            z = z_order(i)
            z_arrival(a, z).wait_recv()
            send_own(a, z)

    slots = lax.broadcasted_iota(jnp.int32, list_v.shape, 1) + 1
    most = jnp.max(jnp.where(list_v[...] >= 0, slots, 0), axis=1)
    used = jnp.max(most, axis=0, keepdims=True).astype(jnp.float32)
    across = lax.broadcasted_iota(jnp.int32, (H, H), 1)
    down = lax.broadcasted_iota(jnp.int32, (H, H), 0)
    other = jnp.broadcast_to(used, (H, H))
    mine = jnp.sum(jnp.where(across == down, other, 0.0), axis=1, keepdims=True)
    ahead = jnp.logical_or(other > mine, jnp.logical_and(other == mine, across < down))
    ahead = jnp.logical_and(ahead, across // heads == down // heads)
    rank = jnp.sum(jnp.where(ahead, 1.0, 0.0), axis=1, keepdims=True)
    holds = jnp.logical_and(rank == across.astype(jnp.float32), down // heads == m)
    order = jnp.sum(jnp.where(holds, (down - m * heads).astype(jnp.float32), 0.0), axis=0, keepdims=True)
    plan_row = lax.broadcasted_iota(jnp.int32, plan.shape, 0)
    plan[...] = jnp.where(plan_row == 0, used, order).astype(jnp.int32)

    spread = (lax.broadcasted_iota(jnp.int32, (kmax, kmax * BLK), 1) // BLK
              == lax.broadcasted_iota(jnp.int32, (kmax, kmax * BLK), 0)).astype(jnp.bfloat16)
    inside = (lax.broadcasted_iota(jnp.int32, (heads, kmax * BLK), 1) % BLK).astype(jnp.float32)
    for qb in range(q_blocks):
        named = list_v[qb].astype(jnp.float32).astype(jnp.bfloat16)
        spaced[...] = lax.dot_general(
            named, spread, (((0,), (0,)), ((), ())), preferred_element_type=jnp.float32)
        block = spaced[pl.ds(pl.multiple_of(m * heads, heads), heads), :]
        kpos[qb] = jnp.where(block < 0, FAR, block * BLK + inside)

    @pl.loop(0, n_mlp)
    def _(i):
        pass_on(0, z_order(i))

    finish(0)
    q_copy.wait()

    factor = math.log2(math.e) / math.sqrt(HD)
    first = s * q_blocks * BLK
    parts = [slice(qb * BLK, (qb + 1) * BLK) for qb in range(q_blocks)]
    row_in_block = lax.broadcasted_iota(jnp.int32, (BLK, 1), 0)
    steps = heads // together

    def p_copy(t):
        some = pl.ds(t * together, together)
        return pltpu.make_async_copy(probs.at[some], p_out.at[some], p_sem.at[t])

    @pl.loop(0, steps)
    def _(t):
        scores = {}

        def score(h, j):
            for qb in range(q_blocks):
                names = [jnp.maximum(list_s[qb, k, m * heads + h], 0) for k in range(kmax)]
                keys = jnp.concatenate([kbuf[b, :, lanes(h // PER_GROUP)] for b in names], axis=0)
                scores[j, qb] = lax.dot_general(
                    qbuf[parts[qb], lanes(h)], keys, (((1,), (1,)), ((), ())),
                    preferred_element_type=jnp.float32)

        def weigh(h, j):
            for qb in range(q_blocks):
                row = (row_in_block + (first + qb * BLK)).astype(jnp.float32)
                masked = jnp.where(kpos[qb, pl.ds(h, 1), :] <= row, scores.pop((j, qb)), MASKED)
                top = jnp.max(masked, axis=1, keepdims=True)
                raised = jnp.exp2((masked - top) * factor)
                scale = 1.0 / jnp.sum(raised, axis=1, keepdims=True)
                probs[h, parts[qb], :] = (raised * scale).astype(probs.dtype)

        for j in range(together + 1):
            if j > 0:
                weigh(t * together + j - 1, j - 1)
            if j < together:
                score(t * together + j, j)
        p_copy(t).start()
        if steps == n_mlp:
            pass_on(1, z_order(t))

    if steps != n_mlp:
        @pl.loop(0, n_mlp)
        def _(i):
            pass_on(1, z_order(i))

    finish(1)

    @pl.loop(0, steps)
    def _(t):
        p_copy(t).wait()

    for a in range(2):
        @pl.loop(1, n_mlp)
        def _(i):
            z_copy(a, z_order(i)).wait_send()

        @pl.loop(0, n_mlp)
        def _(z):
            @pl.loop(p + 1, chips)
            def _(to_p):
                own_copy(a, z, to_p).wait_send()

            @pl.when(c == 0)
            def _():
                own_sib_copy(a, z).wait_send()

            @pl.loop(0, p)
            def _(src_p):
                sib_copy(a, z, src_p).wait_send()


def combine_kernel(
    list_hbm, plan_hbm, p_hbm, v_hbm, out_hbm, listing, plan, pbuf, vbuf, out_buf, sem, p_sem, out_sem,
):
    m = lax.axis_index("mlp")
    q_blocks, kmax = listing.shape[:2]
    heads = pbuf.shape[0]
    together = 4 if kmax <= 16 else 1
    parts = [slice(qb * BLK, (qb + 1) * BLK) for qb in range(q_blocks)]

    plan_copy = pltpu.make_async_copy(plan_hbm, plan, sem.at[0])
    copies = [
        pltpu.make_async_copy(list_hbm, listing, sem.at[1]),
        pltpu.make_async_copy(v_hbm, vbuf, sem.at[2]),
    ]
    plan_copy.start()
    for copy in copies:
        copy.start()

    def p_copy(h):
        return pltpu.make_async_copy(p_hbm.at[h], pbuf.at[h], p_sem.at[h])

    def out_copy(h):
        return pltpu.make_async_copy(out_buf.at[:, lanes(h)], out_hbm.at[:, lanes(h)], out_sem.at[h])

    plan_copy.wait()

    @pl.loop(0, heads)
    def _(i):
        p_copy(plan[1, i]).start()

    def combine(members, count):
        for h in members:
            for qb in range(q_blocks):
                names = [jnp.maximum(listing[qb, k, m * heads + h], 0) for k in range(count)]
                values = jnp.concatenate([vbuf[b, :, lanes(h // PER_GROUP)] for b in names], axis=0)
                product = jnp.dot(
                    pbuf[h, parts[qb], :count * BLK], values, preferred_element_type=jnp.float32)
                out_buf[parts[qb], lanes(h)] = product.astype(out_buf.dtype)

    for copy in copies:
        copy.wait()
    steps = [kmax * i // 4 for i in range(1, 5)]

    @pl.loop(0, heads // together)
    def _(t):
        members = [plan[1, t * together + j] for j in range(together)]
        need = plan[0, m * heads + members[0]]
        for h in members:
            p_copy(h).wait()
        for below, high in zip([0] + steps, steps):
            @pl.when(jnp.logical_and(need > below, need <= high))
            def _():
                combine(members, high)

        for h in members:
            out_copy(h).start()

    @pl.loop(0, heads)
    def _(h):
        out_copy(h).wait()


def body(n_seq, n_mlp, query_rows, key_rows, value_rows, key_blocks):
    piece = key_rows.shape[0]
    rows = query_rows.shape[0]
    heads = H // n_mlp
    width = (KVH // n_mlp) * HD
    q_blocks, kmax = key_blocks.shape[1:]
    chips = n_seq // 2
    blocks = n_seq * n_mlp
    listing = jnp.transpose(key_blocks, (1, 2, 0))
    dma = pltpu.SemaphoreType.DMA
    whole = pl.BlockSpec(memory_space=pltpu.VMEM)
    anywhere = pl.BlockSpec(memory_space=pl.ANY)
    scalars = pl.BlockSpec(memory_space=pltpu.SMEM)
    room = 62 * 1024 * 1024
    values, probs, plan = pl.pallas_call(
        functools.partial(score_kernel, n_seq, n_mlp),
        out_shape=(
            jax.ShapeDtypeStruct((blocks, piece, width), jnp.bfloat16),
            jax.ShapeDtypeStruct((heads, rows, kmax * BLK), jnp.bfloat16),
            jax.ShapeDtypeStruct((8, H), jnp.int32),
        ),
        in_specs=[scalars, whole, anywhere, anywhere, anywhere],
        out_specs=(anywhere, anywhere, whole),
        scratch_shapes=[
            pltpu.VMEM((blocks, piece, width), jnp.bfloat16),
            pltpu.VMEM((rows, heads * HD), jnp.bfloat16),
            pltpu.VMEM((q_blocks, heads, kmax * BLK), jnp.float32),
            pltpu.VMEM((H, kmax * BLK), jnp.float32),
            pltpu.VMEM((heads, rows, kmax * BLK), jnp.bfloat16),
            dma((3,)),
            dma((heads,)),
            dma((2, n_mlp)),
            dma((2, n_mlp)),
            dma((2, n_mlp, chips)),
            dma((2, n_mlp, chips)),
            dma((2, n_mlp)),
            dma((2, n_mlp, chips)),
            dma((2, n_mlp, chips)),
        ],
        compiler_params=pltpu.CompilerParams(
            collective_id=0, has_side_effects=True, vmem_limit_bytes=room),
        name="gather_and_score",
    )(listing, listing, query_rows, key_rows, value_rows)
    return pl.pallas_call(
        combine_kernel,
        out_shape=jax.ShapeDtypeStruct((rows, heads * HD), jnp.bfloat16),
        in_specs=[anywhere] * 4,
        out_specs=anywhere,
        scratch_shapes=[
            pltpu.SMEM((q_blocks, kmax, H), jnp.int32),
            pltpu.SMEM((8, H), jnp.int32),
            pltpu.VMEM((heads, rows, kmax * BLK), jnp.bfloat16),
            pltpu.VMEM((blocks, piece, width), jnp.bfloat16),
            pltpu.VMEM((rows, heads * HD), jnp.bfloat16),
            dma((3,)),
            dma((heads,)),
            dma((heads,)),
        ],
        compiler_params=pltpu.CompilerParams(vmem_limit_bytes=room),
        name="combine_listed_values",
    )(listing, plan, probs, values)


def solution(mesh):
    placed = (
        P("seq", None),
        P(("seq", "mlp"), None),
        P(("seq", "mlp"), None),
        P(None, "seq", None),
    )
    return jax.shard_map(
        functools.partial(body, mesh.shape["seq"], mesh.shape["mlp"]),
        mesh=mesh, in_specs=placed, out_specs=P("seq", "mlp"), check_vma=False
    )
```

```python
import functools
import math

import jax
import jax.numpy as jnp
from jax import lax
from jax.experimental import pallas as pl
from jax.experimental.pallas import tpu as pltpu
from jax.sharding import PartitionSpec as P

H = 64
KVH = 8
HD = 128
BLK = 64
PER_GROUP = H // KVH

MESH = pl.DeviceIdType.MESH
MASKED = -1e30
FAR = 1e9


def lanes(index, size=HD):
    return pl.ds(pl.multiple_of(index * size, size), size)


def score_kernel(
    n_seq, n_mlp, list_s, list_v, q_hbm, k_hbm, v_hbm, v_out, p_out, k_out, kpos_out, plan,
    kbuf, qbuf, kpos, spaced, probs,
    local_sem, p_sem, z_send, z_recv, hop_send, hop_recv, own_sib_send, sib_send, sib_recv,
):
    s = lax.axis_index("seq")
    m = lax.axis_index("mlp")
    chips = n_seq // 2
    p, c = s // 2, s % 2
    width = kbuf.shape[2]
    q_blocks, kmax = list_v.shape[:2]
    heads = H // n_mlp
    half = heads // 2
    together = 4 if kmax <= 16 else 1
    srcs = (k_hbm, v_hbm)
    bufs = (kbuf, v_out)
    sibling = 2 * p + 1 - c

    def z_copy(a, to):
        return pltpu.make_async_remote_copy(
            src_ref=srcs[a].at[:, lanes(to, width)], dst_ref=bufs[a].at[s * n_mlp + m],
            send_sem=z_send.at[a, to], recv_sem=z_recv.at[a, m],
            device_id=(s, to), device_id_type=MESH)

    def z_arrival(a, z):
        return pltpu.make_async_remote_copy(
            src_ref=srcs[a].at[:, lanes(z, width)], dst_ref=bufs[a].at[s * n_mlp + z],
            send_sem=z_send.at[a, z], recv_sem=z_recv.at[a, z],
            device_id=(s, z), device_id_type=MESH)

    def moved(a, src_p, src_c, z, to_s, send, recv):
        part = bufs[a].at[(2 * src_p + src_c) * n_mlp + z]
        return pltpu.make_async_remote_copy(
            src_ref=part, dst_ref=part, send_sem=send, recv_sem=recv,
            device_id=(to_s, m), device_id_type=MESH)

    def own_copy(a, z, to_p):
        return moved(a, p, c, z, 2 * to_p + c, hop_send.at[a, z, to_p], hop_recv.at[a, z, p])

    def hop_arrival(a, z, src_p):
        return moved(a, src_p, c, z, 2 * src_p + c, hop_send.at[a, z, src_p], hop_recv.at[a, z, src_p])

    def own_sib_copy(a, z):
        return moved(a, p, c, z, sibling, own_sib_send.at[a, z], sib_recv.at[a, z, p])

    def sib_copy(a, z, src_p):
        return moved(a, src_p, c, z, sibling, sib_send.at[a, z, src_p], sib_recv.at[a, z, src_p])

    def sib_arrival(a, z, src_p):
        return moved(a, src_p, 1 - c, z, sibling, sib_send.at[a, z, src_p], sib_recv.at[a, z, src_p])

    def send_own(a, z):
        @pl.loop(p + 1, chips)
        def _(to_p):
            own_copy(a, z, to_p).start()

        @pl.when(c == 0)
        def _():
            own_sib_copy(a, z).start()

    def pass_on(a, z):
        @pl.loop(0, p)
        def _(src_p):
            hop_arrival(a, z, src_p).wait_recv()
            sib_copy(a, z, src_p).start()

    def finish(a):
        @pl.loop(0, n_mlp)
        def _(z):
            @pl.loop(0, p + c)
            def _(src_p):
                sib_arrival(a, z, src_p).wait_recv()

    def z_order(i):
        if n_mlp != 4:
            return lax.rem(m + i, n_mlp)
        second = jnp.where(jnp.logical_or(m == 0, m == 2), 1, 2)
        third = jnp.where(m == 0, 2, jnp.where(m == 1, 0, jnp.where(m == 2, 3, 1)))
        last = jnp.where(m < 2, 3, 0)
        return jnp.where(i == 0, m, jnp.where(i == 1, second, jnp.where(i == 2, third, last)))

    def local_copy(a):
        return pltpu.make_async_copy(
            srcs[a].at[:, lanes(m, width)], bufs[a].at[s * n_mlp + m], local_sem.at[a])

    q_copy = pltpu.make_async_copy(q_hbm.at[:, lanes(2 * m, half * HD)], qbuf, local_sem.at[2])
    local_copy(0).start()
    local_copy(1).start()

    barrier = pltpu.get_barrier_semaphore()

    @pl.loop(1, n_mlp)
    def _(i):
        pl.semaphore_signal(barrier, inc=1, device_id=(s, z_order(i)), device_id_type=MESH)

    @pl.loop(1, chips)
    def _(i):
        pl.semaphore_signal(
            barrier, inc=1, device_id=(2 * lax.rem(p + i, chips) + c, m), device_id_type=MESH)

    pl.semaphore_signal(barrier, inc=1, device_id=(sibling, m), device_id_type=MESH)
    pl.semaphore_wait(barrier, n_mlp - 1 + chips - 1 + 1)

    for a in range(2):
        @pl.loop(1, n_mlp)
        def _(i):
            z_copy(a, z_order(i)).start()

    q_copy.start()
    for a in range(2):
        local_copy(a).wait()
        send_own(a, m)

        @pl.loop(1, n_mlp)
        def _(i):
            z = z_order(i)
            z_arrival(a, z).wait_recv()
            send_own(a, z)

    slots = lax.broadcasted_iota(jnp.int32, list_v.shape, 1) + 1
    most = jnp.max(jnp.where(list_v[...] >= 0, slots, 0), axis=1)
    used = jnp.max(most, axis=0, keepdims=True).astype(jnp.float32)
    across = lax.broadcasted_iota(jnp.int32, (H, H), 1)
    down = lax.broadcasted_iota(jnp.int32, (H, H), 0)
    other = jnp.broadcast_to(used, (H, H))
    mine = jnp.sum(jnp.where(across == down, other, 0.0), axis=1, keepdims=True)
    ahead = jnp.logical_or(other > mine, jnp.logical_and(other == mine, across < down))
    ahead = jnp.logical_and(ahead, across // half == down // half)
    rank = jnp.sum(jnp.where(ahead, 1.0, 0.0), axis=1, keepdims=True)
    local = (down - m * heads).astype(jnp.float32)

    def order(which):
        holds = jnp.logical_and(rank == across.astype(jnp.float32), down // half == 2 * m + which)
        return jnp.sum(jnp.where(holds, local, 0.0), axis=0, keepdims=True)

    plan_row = lax.broadcasted_iota(jnp.int32, plan.shape, 0)
    rows = jnp.where(plan_row == 0, used, jnp.where(plan_row == 1, order(0), order(1)))
    plan[...] = rows.astype(jnp.int32)

    spread = (lax.broadcasted_iota(jnp.int32, (kmax, kmax * BLK), 1) // BLK
              == lax.broadcasted_iota(jnp.int32, (kmax, kmax * BLK), 0)).astype(jnp.bfloat16)
    inside = (lax.broadcasted_iota(jnp.int32, (half, kmax * BLK), 1) % BLK).astype(jnp.float32)
    for qb in range(q_blocks):
        named = list_v[qb].astype(jnp.float32).astype(jnp.bfloat16)
        spaced[...] = lax.dot_general(
            named, spread, (((0,), (0,)), ((), ())), preferred_element_type=jnp.float32)
        for which, target in enumerate((kpos, kpos_out)):
            block = spaced[pl.ds(pl.multiple_of((2 * m + which) * half, half), half), :]
            target[qb] = jnp.where(block < 0, FAR, block * BLK + inside)

    @pl.loop(0, n_mlp)
    def _(i):
        pass_on(0, z_order(i))

    finish(0)
    k_copy = pltpu.make_async_copy(kbuf.at[:, :, width // 2:], k_out, local_sem.at[3])
    k_copy.start()
    q_copy.wait()

    factor = math.log2(math.e) / math.sqrt(HD)
    first = s * q_blocks * BLK
    parts = [slice(qb * BLK, (qb + 1) * BLK) for qb in range(q_blocks)]
    row_in_block = lax.broadcasted_iota(jnp.int32, (BLK, 1), 0)
    steps = half // together
    per = max(n_mlp // steps, 1)

    def p_copy(t):
        some = pl.ds(t * together, together)
        return pltpu.make_async_copy(probs.at[some], p_out.at[some], p_sem.at[t])

    @pl.loop(0, steps)
    def _(t):
        scores = {}

        def score(h, j):
            for qb in range(q_blocks):
                names = [jnp.maximum(list_s[qb, k, m * heads + h], 0) for k in range(kmax)]
                keys = jnp.concatenate([kbuf[b, :, lanes(h // PER_GROUP)] for b in names], axis=0)
                scores[j, qb] = lax.dot_general(
                    qbuf[parts[qb], lanes(h)], keys, (((1,), (1,)), ((), ())),
                    preferred_element_type=jnp.float32)

        def weigh(h, j):
            for qb in range(q_blocks):
                row = (row_in_block + (first + qb * BLK)).astype(jnp.float32)
                masked = jnp.where(kpos[qb, pl.ds(h, 1), :] <= row, scores.pop((j, qb)), MASKED)
                top = jnp.max(masked, axis=1, keepdims=True)
                raised = jnp.exp2((masked - top) * factor)
                scale = 1.0 / jnp.sum(raised, axis=1, keepdims=True)
                probs[h, parts[qb], :] = (raised * scale).astype(probs.dtype)

        for j in range(together + 1):
            if j > 0:
                weigh(t * together + j - 1, j - 1)
            if j < together:
                score(t * together + j, j)
        p_copy(t).start()
        if per * steps == n_mlp:
            for i in range(per):
                pass_on(1, z_order(t * per + i))

    if per * steps != n_mlp:
        @pl.loop(0, n_mlp)
        def _(i):
            pass_on(1, z_order(i))

    finish(1)

    @pl.loop(0, steps)
    def _(t):
        p_copy(t).wait()

    k_copy.wait()

    for a in range(2):
        @pl.loop(1, n_mlp)
        def _(i):
            z_copy(a, z_order(i)).wait_send()

        @pl.loop(0, n_mlp)
        def _(z):
            @pl.loop(p + 1, chips)
            def _(to_p):
                own_copy(a, z, to_p).wait_send()

            @pl.when(c == 0)
            def _():
                own_sib_copy(a, z).wait_send()

            @pl.loop(0, p)
            def _(src_p):
                sib_copy(a, z, src_p).wait_send()


def finish_kernel(
    list_hbm, plan_hbm, kpos, p_hbm, k_hbm, v_hbm, q_hbm, out_hbm,
    listing, plan, pbuf, kbuf, vbuf, qbuf, out_buf, sem, p_sem, out_sem,
):
    s = lax.axis_index("seq")
    m = lax.axis_index("mlp")
    q_blocks, kmax = listing.shape[:2]
    half = pbuf.shape[0]
    heads = 2 * half
    base = half // PER_GROUP
    together = 4 if kmax <= 16 else 1
    factor = math.log2(math.e) / math.sqrt(HD)
    first = s * q_blocks * BLK
    parts = [slice(qb * BLK, (qb + 1) * BLK) for qb in range(q_blocks)]
    row_in_block = lax.broadcasted_iota(jnp.int32, (BLK, 1), 0)

    copies = [
        pltpu.make_async_copy(plan_hbm, plan, sem.at[0]),
        pltpu.make_async_copy(list_hbm, listing, sem.at[1]),
        pltpu.make_async_copy(q_hbm.at[:, lanes(2 * m + 1, half * HD)], qbuf, sem.at[2]),
        pltpu.make_async_copy(k_hbm, kbuf, sem.at[3]),
        pltpu.make_async_copy(v_hbm, vbuf, sem.at[4]),
    ]
    for copy in copies:
        copy.start()

    def p_copy(h):
        return pltpu.make_async_copy(p_hbm.at[h], pbuf.at[h], p_sem.at[h])

    def out_copy(h):
        return pltpu.make_async_copy(out_buf.at[:, lanes(h)], out_hbm.at[:, lanes(h)], out_sem.at[h])

    @pl.loop(0, half)
    def _(h):
        p_copy(h).start()

    def attend(members, count):
        places = [
            [[jnp.maximum(listing[qb, k, m * heads + h], 0) for k in range(count)]
             for qb in range(q_blocks)] for h in members]
        scores, weights, totals = {}, {}, {}

        def gathered(buf, j, qb):
            group = lanes(members[j] // PER_GROUP - base) if buf is kbuf else lanes(members[j] // PER_GROUP)
            return jnp.concatenate([buf[b, :, group] for b in places[j][qb]], axis=0)

        def score(j):
            for qb in range(q_blocks):
                scores[j, qb] = lax.dot_general(
                    qbuf[parts[qb], lanes(members[j] - half)], gathered(kbuf, j, qb), (((1,), (1,)), ((), ())),
                    preferred_element_type=jnp.float32)

        def weigh(j):
            for qb in range(q_blocks):
                row = (row_in_block + (first + qb * BLK)).astype(jnp.float32)
                position = kpos[qb, pl.ds(members[j] - half, 1), :count * BLK]
                masked = jnp.where(position <= row, scores.pop((j, qb)), MASKED)
                top = jnp.max(masked, axis=1, keepdims=True)
                raised = jnp.exp2((masked - top) * factor)
                totals[j, qb] = jnp.sum(raised, axis=1, keepdims=True)
                weights[j, qb] = raised.astype(jnp.bfloat16)

        def combine(j):
            for qb in range(q_blocks):
                product = jnp.dot(
                    weights.pop((j, qb)), gathered(vbuf, j, qb), preferred_element_type=jnp.float32)
                out_buf[parts[qb], lanes(members[j])] = (product / totals.pop((j, qb))).astype(out_buf.dtype)

        for step in range(len(members) + 2):
            for stage, lag in ((combine, 2), (weigh, 1), (score, 0)):
                if 0 <= step - lag < len(members):
                    stage(step - lag)

    def apply(members, count):
        for h in members:
            for qb in range(q_blocks):
                names = [jnp.maximum(listing[qb, k, m * heads + h], 0) for k in range(count)]
                values = jnp.concatenate([vbuf[b, :, lanes(h // PER_GROUP)] for b in names], axis=0)
                product = jnp.dot(
                    pbuf[h, parts[qb], :count * BLK], values, preferred_element_type=jnp.float32)
                out_buf[parts[qb], lanes(h)] = product.astype(out_buf.dtype)

    for copy in copies:
        copy.wait()
    steps = [kmax * i // 4 for i in range(1, 5)]

    def run(act, row):
        @pl.loop(0, half // together)
        def _(t):
            members = [plan[row, t * together + j] for j in range(together)]
            need = plan[0, m * heads + members[0]]
            for below, high in zip([0] + steps, steps):
                @pl.when(jnp.logical_and(need > below, need <= high))
                def _():
                    act(members, high)

            for h in members:
                out_copy(h).start()

    run(attend, 2)

    @pl.loop(0, half)
    def _(h):
        p_copy(h).wait()

    run(apply, 1)

    @pl.loop(0, heads)
    def _(h):
        out_copy(h).wait()


def body(n_seq, n_mlp, query_rows, key_rows, value_rows, key_blocks):
    piece = key_rows.shape[0]
    rows = query_rows.shape[0]
    heads = H // n_mlp
    half = heads // 2
    width = (KVH // n_mlp) * HD
    q_blocks, kmax = key_blocks.shape[1:]
    chips = n_seq // 2
    blocks = n_seq * n_mlp
    listing = jnp.transpose(key_blocks, (1, 2, 0))
    dma = pltpu.SemaphoreType.DMA
    whole = pl.BlockSpec(memory_space=pltpu.VMEM)
    anywhere = pl.BlockSpec(memory_space=pl.ANY)
    scalars = pl.BlockSpec(memory_space=pltpu.SMEM)
    room = 62 * 1024 * 1024
    values, probs, keys, kpos, plan = pl.pallas_call(
        functools.partial(score_kernel, n_seq, n_mlp),
        out_shape=(
            jax.ShapeDtypeStruct((blocks, piece, width), jnp.bfloat16),
            jax.ShapeDtypeStruct((half, rows, kmax * BLK), jnp.bfloat16),
            jax.ShapeDtypeStruct((blocks, piece, width // 2), jnp.bfloat16),
            jax.ShapeDtypeStruct((q_blocks, half, kmax * BLK), jnp.float32),
            jax.ShapeDtypeStruct((8, H), jnp.int32),
        ),
        in_specs=[scalars, whole, anywhere, anywhere, anywhere],
        out_specs=(anywhere, anywhere, anywhere, whole, whole),
        scratch_shapes=[
            pltpu.VMEM((blocks, piece, width), jnp.bfloat16),
            pltpu.VMEM((rows, half * HD), jnp.bfloat16),
            pltpu.VMEM((q_blocks, half, kmax * BLK), jnp.float32),
            pltpu.VMEM((H, kmax * BLK), jnp.float32),
            pltpu.VMEM((half, rows, kmax * BLK), jnp.bfloat16),
            dma((4,)),
            dma((half,)),
            dma((2, n_mlp)),
            dma((2, n_mlp)),
            dma((2, n_mlp, chips)),
            dma((2, n_mlp, chips)),
            dma((2, n_mlp)),
            dma((2, n_mlp, chips)),
            dma((2, n_mlp, chips)),
        ],
        compiler_params=pltpu.CompilerParams(
            collective_id=0, has_side_effects=True, vmem_limit_bytes=room),
        name="gather_and_score",
    )(listing, listing, query_rows, key_rows, value_rows)
    return pl.pallas_call(
        finish_kernel,
        out_shape=jax.ShapeDtypeStruct((rows, heads * HD), jnp.bfloat16),
        in_specs=[anywhere, anywhere, whole, anywhere, anywhere, anywhere, anywhere],
        out_specs=anywhere,
        scratch_shapes=[
            pltpu.SMEM((q_blocks, kmax, H), jnp.int32),
            pltpu.SMEM((8, H), jnp.int32),
            pltpu.VMEM((half, rows, kmax * BLK), jnp.bfloat16),
            pltpu.VMEM((blocks, piece, width // 2), jnp.bfloat16),
            pltpu.VMEM((blocks, piece, width), jnp.bfloat16),
            pltpu.VMEM((rows, half * HD), jnp.bfloat16),
            pltpu.VMEM((rows, heads * HD), jnp.bfloat16),
            dma((5,)),
            dma((half,)),
            dma((heads,)),
        ],
        compiler_params=pltpu.CompilerParams(vmem_limit_bytes=room),
        name="attend_and_combine",
    )(listing, plan, kpos, probs, keys, values, query_rows)


def solution(mesh):
    placed = (
        P("seq", None),
        P(("seq", "mlp"), None),
        P(("seq", "mlp"), None),
        P(None, "seq", None),
    )
    return jax.shard_map(
        functools.partial(body, mesh.shape["seq"], mesh.shape["mlp"]),
        mesh=mesh, in_specs=placed, out_specs=P("seq", "mlp"), check_vma=False
    )
```

```python
import functools
import math

import jax
import jax.numpy as jnp
from jax import lax
from jax.experimental import pallas as pl
from jax.experimental.pallas import tpu as pltpu
from jax.sharding import PartitionSpec as P

H = 64
KVH = 8
HD = 128
BLK = 64
PER_GROUP = H // KVH

MESH = pl.DeviceIdType.MESH
MASKED = -1e30
FAR = 1e9


def lanes(index, size=HD):
    return pl.ds(pl.multiple_of(index * size, size), size)


def score_kernel(
    n_seq, n_mlp, list_s, list_v, q_hbm, k_hbm, v_hbm, v_out, p_out, k_out, kpos_out, plan,
    kbuf, qbuf, kpos, spaced, probs,
    local_sem, p_sem, z_send, z_recv, hop_send, hop_recv, own_sib_send, sib_send, sib_recv,
):
    s = lax.axis_index("seq")
    m = lax.axis_index("mlp")
    chips = n_seq // 2
    p, c = s // 2, s % 2
    width = kbuf.shape[2]
    q_blocks, kmax = list_v.shape[:2]
    heads = H // n_mlp
    half = heads // 2
    together = 4 if kmax <= 16 else 1
    srcs = (k_hbm, v_hbm)
    bufs = (kbuf, v_out)
    sibling = 2 * p + 1 - c

    def z_copy(a, to):
        return pltpu.make_async_remote_copy(
            src_ref=srcs[a].at[:, lanes(to, width)], dst_ref=bufs[a].at[s * n_mlp + m],
            send_sem=z_send.at[a, to], recv_sem=z_recv.at[a, m],
            device_id=(s, to), device_id_type=MESH)

    def z_arrival(a, z):
        return pltpu.make_async_remote_copy(
            src_ref=srcs[a].at[:, lanes(z, width)], dst_ref=bufs[a].at[s * n_mlp + z],
            send_sem=z_send.at[a, z], recv_sem=z_recv.at[a, z],
            device_id=(s, z), device_id_type=MESH)

    def moved(a, src_p, src_c, z, to_s, send, recv):
        part = bufs[a].at[(2 * src_p + src_c) * n_mlp + z]
        return pltpu.make_async_remote_copy(
            src_ref=part, dst_ref=part, send_sem=send, recv_sem=recv,
            device_id=(to_s, m), device_id_type=MESH)

    def own_copy(a, z, to_p):
        return moved(a, p, c, z, 2 * to_p + c, hop_send.at[a, z, to_p], hop_recv.at[a, z, p])

    def hop_arrival(a, z, src_p):
        return moved(a, src_p, c, z, 2 * src_p + c, hop_send.at[a, z, src_p], hop_recv.at[a, z, src_p])

    def own_sib_copy(a, z):
        return moved(a, p, c, z, sibling, own_sib_send.at[a, z], sib_recv.at[a, z, p])

    def sib_copy(a, z, src_p):
        return moved(a, src_p, c, z, sibling, sib_send.at[a, z, src_p], sib_recv.at[a, z, src_p])

    def sib_arrival(a, z, src_p):
        return moved(a, src_p, 1 - c, z, sibling, sib_send.at[a, z, src_p], sib_recv.at[a, z, src_p])

    def send_own(a, z):
        @pl.loop(p + 1, chips)
        def _(to_p):
            own_copy(a, z, to_p).start()

        @pl.when(c == 0)
        def _():
            own_sib_copy(a, z).start()

    def pass_on(a, z):
        @pl.loop(0, p)
        def _(src_p):
            hop_arrival(a, z, src_p).wait_recv()
            sib_copy(a, z, src_p).start()

    def finish(a):
        @pl.loop(0, n_mlp)
        def _(z):
            @pl.loop(0, p + c)
            def _(src_p):
                sib_arrival(a, z, src_p).wait_recv()

    def z_order(i):
        if n_mlp != 4:
            return lax.rem(m + i, n_mlp)
        second = jnp.where(jnp.logical_or(m == 0, m == 2), 1, 2)
        third = jnp.where(m == 0, 2, jnp.where(m == 1, 0, jnp.where(m == 2, 3, 1)))
        last = jnp.where(m < 2, 3, 0)
        return jnp.where(i == 0, m, jnp.where(i == 1, second, jnp.where(i == 2, third, last)))

    def local_copy(a):
        return pltpu.make_async_copy(
            srcs[a].at[:, lanes(m, width)], bufs[a].at[s * n_mlp + m], local_sem.at[a])

    q_copy = pltpu.make_async_copy(q_hbm.at[:, lanes(2 * m, half * HD)], qbuf, local_sem.at[2])
    local_copy(0).start()
    local_copy(1).start()

    barrier = pltpu.get_barrier_semaphore()

    @pl.loop(1, n_mlp)
    def _(i):
        pl.semaphore_signal(barrier, inc=1, device_id=(s, z_order(i)), device_id_type=MESH)

    @pl.loop(1, chips)
    def _(i):
        pl.semaphore_signal(
            barrier, inc=1, device_id=(2 * lax.rem(p + i, chips) + c, m), device_id_type=MESH)

    pl.semaphore_signal(barrier, inc=1, device_id=(sibling, m), device_id_type=MESH)
    pl.semaphore_wait(barrier, n_mlp - 1 + chips - 1 + 1)

    def z_start(a):
        @pl.loop(1, n_mlp)
        def _(i):
            z_copy(a, z_order(i)).start()

    def spread_own(a):
        local_copy(a).wait()
        send_own(a, m)

        @pl.loop(1, n_mlp)
        def _(i):
            z = z_order(i)
            z_arrival(a, z).wait_recv()
            send_own(a, z)

    def own_sent(a):
        @pl.loop(0, n_mlp)
        def _(z):
            @pl.loop(p + 1, chips)
            def _(to_p):
                own_copy(a, z, to_p).wait_send()

    z_start(0)
    q_copy.start()
    spread_own(0)
    z_start(1)

    slots = lax.broadcasted_iota(jnp.int32, list_v.shape, 1) + 1
    most = jnp.max(jnp.where(list_v[...] >= 0, slots, 0), axis=1)
    used = jnp.max(most, axis=0, keepdims=True).astype(jnp.float32)
    across = lax.broadcasted_iota(jnp.int32, (H, H), 1)
    down = lax.broadcasted_iota(jnp.int32, (H, H), 0)
    other = jnp.broadcast_to(used, (H, H))
    mine = jnp.sum(jnp.where(across == down, other, 0.0), axis=1, keepdims=True)
    ahead = jnp.logical_or(other > mine, jnp.logical_and(other == mine, across < down))
    ahead = jnp.logical_and(ahead, across // half == down // half)
    rank = jnp.sum(jnp.where(ahead, 1.0, 0.0), axis=1, keepdims=True)
    local = (down - m * heads).astype(jnp.float32)

    def order(which):
        holds = jnp.logical_and(rank == across.astype(jnp.float32), down // half == 2 * m + which)
        return jnp.sum(jnp.where(holds, local, 0.0), axis=0, keepdims=True)

    plan_row = lax.broadcasted_iota(jnp.int32, plan.shape, 0)
    rows = jnp.where(plan_row == 0, used, jnp.where(plan_row == 1, order(0), order(1)))
    plan[...] = rows.astype(jnp.int32)

    spread = (lax.broadcasted_iota(jnp.int32, (kmax, kmax * BLK), 1) // BLK
              == lax.broadcasted_iota(jnp.int32, (kmax, kmax * BLK), 0)).astype(jnp.bfloat16)
    inside = (lax.broadcasted_iota(jnp.int32, (half, kmax * BLK), 1) % BLK).astype(jnp.float32)
    for qb in range(q_blocks):
        named = list_v[qb].astype(jnp.float32).astype(jnp.bfloat16)
        spaced[...] = lax.dot_general(
            named, spread, (((0,), (0,)), ((), ())), preferred_element_type=jnp.float32)
        for which, target in enumerate((kpos, kpos_out)):
            block = spaced[pl.ds(pl.multiple_of((2 * m + which) * half, half), half), :]
            target[qb] = jnp.where(block < 0, FAR, block * BLK + inside)

    @pl.loop(0, n_mlp)
    def _(i):
        pass_on(0, z_order(i))

    own_sent(0)
    spread_own(1)
    finish(0)
    k_copy = pltpu.make_async_copy(kbuf.at[:, :, width // 2:], k_out, local_sem.at[3])
    k_copy.start()
    q_copy.wait()

    factor = math.log2(math.e) / math.sqrt(HD)
    first = s * q_blocks * BLK
    parts = [slice(qb * BLK, (qb + 1) * BLK) for qb in range(q_blocks)]
    row_in_block = lax.broadcasted_iota(jnp.int32, (BLK, 1), 0)
    steps = half // together
    per = max(n_mlp // steps, 1)

    def p_copy(t):
        some = pl.ds(t * together, together)
        return pltpu.make_async_copy(probs.at[some], p_out.at[some], p_sem.at[t])

    @pl.loop(0, steps)
    def _(t):
        scores = {}

        def score(h, j):
            for qb in range(q_blocks):
                names = [jnp.maximum(list_s[qb, k, m * heads + h], 0) for k in range(kmax)]
                keys = jnp.concatenate([kbuf[b, :, lanes(h // PER_GROUP)] for b in names], axis=0)
                scores[j, qb] = lax.dot_general(
                    qbuf[parts[qb], lanes(h)], keys, (((1,), (1,)), ((), ())),
                    preferred_element_type=jnp.float32)

        def weigh(h, j):
            for qb in range(q_blocks):
                row = (row_in_block + (first + qb * BLK)).astype(jnp.float32)
                masked = jnp.where(kpos[qb, pl.ds(h, 1), :] <= row, scores.pop((j, qb)), MASKED)
                top = jnp.max(masked, axis=1, keepdims=True)
                raised = jnp.exp2((masked - top) * factor)
                scale = 1.0 / jnp.sum(raised, axis=1, keepdims=True)
                probs[h, parts[qb], :] = (raised * scale).astype(probs.dtype)

        for j in range(together + 1):
            if j > 0:
                weigh(t * together + j - 1, j - 1)
            if j < together:
                score(t * together + j, j)
        p_copy(t).start()
        if per * steps == n_mlp:
            for i in range(per):
                pass_on(1, z_order(t * per + i))

    if per * steps != n_mlp:
        @pl.loop(0, n_mlp)
        def _(i):
            pass_on(1, z_order(i))

    finish(1)

    @pl.loop(0, steps)
    def _(t):
        p_copy(t).wait()

    k_copy.wait()

    for a in range(2):
        @pl.loop(1, n_mlp)
        def _(i):
            z_copy(a, z_order(i)).wait_send()

        if a == 1:
            own_sent(1)

        @pl.loop(0, n_mlp)
        def _(z):
            @pl.when(c == 0)
            def _():
                own_sib_copy(a, z).wait_send()

            @pl.loop(0, p)
            def _(src_p):
                sib_copy(a, z, src_p).wait_send()


def finish_kernel(
    list_hbm, plan_hbm, kpos, p_hbm, k_hbm, v_hbm, q_hbm, out_hbm,
    listing, plan, pbuf, kbuf, vbuf, qbuf, out_buf, sem, p_sem, out_sem,
):
    s = lax.axis_index("seq")
    m = lax.axis_index("mlp")
    q_blocks, kmax = listing.shape[:2]
    half = pbuf.shape[0]
    heads = 2 * half
    base = half // PER_GROUP
    together = 4 if kmax <= 16 else 1
    factor = math.log2(math.e) / math.sqrt(HD)
    first = s * q_blocks * BLK
    parts = [slice(qb * BLK, (qb + 1) * BLK) for qb in range(q_blocks)]
    row_in_block = lax.broadcasted_iota(jnp.int32, (BLK, 1), 0)

    copies = [
        pltpu.make_async_copy(plan_hbm, plan, sem.at[0]),
        pltpu.make_async_copy(list_hbm, listing, sem.at[1]),
        pltpu.make_async_copy(q_hbm.at[:, lanes(2 * m + 1, half * HD)], qbuf, sem.at[2]),
        pltpu.make_async_copy(k_hbm, kbuf, sem.at[3]),
        pltpu.make_async_copy(v_hbm, vbuf, sem.at[4]),
    ]
    for copy in copies:
        copy.start()

    def p_copy(h):
        return pltpu.make_async_copy(p_hbm.at[h], pbuf.at[h], p_sem.at[h])

    def out_copy(h):
        return pltpu.make_async_copy(out_buf.at[:, lanes(h)], out_hbm.at[:, lanes(h)], out_sem.at[h])

    @pl.loop(0, half)
    def _(h):
        p_copy(h).start()

    def attend(members, count):
        places = [
            [[jnp.maximum(listing[qb, k, m * heads + h], 0) for k in range(count)]
             for qb in range(q_blocks)] for h in members]
        scores, weights, totals = {}, {}, {}

        def gathered(buf, j, qb):
            group = lanes(members[j] // PER_GROUP - base) if buf is kbuf else lanes(members[j] // PER_GROUP)
            return jnp.concatenate([buf[b, :, group] for b in places[j][qb]], axis=0)

        def score(j):
            for qb in range(q_blocks):
                scores[j, qb] = lax.dot_general(
                    qbuf[parts[qb], lanes(members[j] - half)], gathered(kbuf, j, qb), (((1,), (1,)), ((), ())),
                    preferred_element_type=jnp.float32)

        def weigh(j):
            for qb in range(q_blocks):
                row = (row_in_block + (first + qb * BLK)).astype(jnp.float32)
                position = kpos[qb, pl.ds(members[j] - half, 1), :count * BLK]
                masked = jnp.where(position <= row, scores.pop((j, qb)), MASKED)
                top = jnp.max(masked, axis=1, keepdims=True)
                raised = jnp.exp2((masked - top) * factor)
                totals[j, qb] = jnp.sum(raised, axis=1, keepdims=True)
                weights[j, qb] = raised.astype(jnp.bfloat16)

        def combine(j):
            for qb in range(q_blocks):
                product = jnp.dot(
                    weights.pop((j, qb)), gathered(vbuf, j, qb), preferred_element_type=jnp.float32)
                out_buf[parts[qb], lanes(members[j])] = (product / totals.pop((j, qb))).astype(out_buf.dtype)

        for step in range(len(members) + 2):
            for stage, lag in ((combine, 2), (weigh, 1), (score, 0)):
                if 0 <= step - lag < len(members):
                    stage(step - lag)

    def apply(members, count):
        for h in members:
            for qb in range(q_blocks):
                names = [jnp.maximum(listing[qb, k, m * heads + h], 0) for k in range(count)]
                values = jnp.concatenate([vbuf[b, :, lanes(h // PER_GROUP)] for b in names], axis=0)
                product = jnp.dot(
                    pbuf[h, parts[qb], :count * BLK], values, preferred_element_type=jnp.float32)
                out_buf[parts[qb], lanes(h)] = product.astype(out_buf.dtype)

    for copy in copies:
        copy.wait()
    steps = [kmax * i // 4 for i in range(1, 5)]

    def run(act, row):
        @pl.loop(0, half // together)
        def _(t):
            members = [plan[row, t * together + j] for j in range(together)]
            need = plan[0, m * heads + members[0]]
            for below, high in zip([0] + steps, steps):
                @pl.when(jnp.logical_and(need > below, need <= high))
                def _():
                    act(members, high)

            for h in members:
                out_copy(h).start()

    run(attend, 2)

    @pl.loop(0, half)
    def _(h):
        p_copy(h).wait()

    run(apply, 1)

    @pl.loop(0, heads)
    def _(h):
        out_copy(h).wait()


def body(n_seq, n_mlp, query_rows, key_rows, value_rows, key_blocks):
    piece = key_rows.shape[0]
    rows = query_rows.shape[0]
    heads = H // n_mlp
    half = heads // 2
    width = (KVH // n_mlp) * HD
    q_blocks, kmax = key_blocks.shape[1:]
    chips = n_seq // 2
    blocks = n_seq * n_mlp
    listing = jnp.transpose(key_blocks, (1, 2, 0))
    dma = pltpu.SemaphoreType.DMA
    whole = pl.BlockSpec(memory_space=pltpu.VMEM)
    anywhere = pl.BlockSpec(memory_space=pl.ANY)
    scalars = pl.BlockSpec(memory_space=pltpu.SMEM)
    room = 62 * 1024 * 1024
    values, probs, keys, kpos, plan = pl.pallas_call(
        functools.partial(score_kernel, n_seq, n_mlp),
        out_shape=(
            jax.ShapeDtypeStruct((blocks, piece, width), jnp.bfloat16),
            jax.ShapeDtypeStruct((half, rows, kmax * BLK), jnp.bfloat16),
            jax.ShapeDtypeStruct((blocks, piece, width // 2), jnp.bfloat16),
            jax.ShapeDtypeStruct((q_blocks, half, kmax * BLK), jnp.float32),
            jax.ShapeDtypeStruct((8, H), jnp.int32),
        ),
        in_specs=[scalars, whole, anywhere, anywhere, anywhere],
        out_specs=(anywhere, anywhere, anywhere, whole, whole),
        scratch_shapes=[
            pltpu.VMEM((blocks, piece, width), jnp.bfloat16),
            pltpu.VMEM((rows, half * HD), jnp.bfloat16),
            pltpu.VMEM((q_blocks, half, kmax * BLK), jnp.float32),
            pltpu.VMEM((H, kmax * BLK), jnp.float32),
            pltpu.VMEM((half, rows, kmax * BLK), jnp.bfloat16),
            dma((4,)),
            dma((half,)),
            dma((2, n_mlp)),
            dma((2, n_mlp)),
            dma((2, n_mlp, chips)),
            dma((2, n_mlp, chips)),
            dma((2, n_mlp)),
            dma((2, n_mlp, chips)),
            dma((2, n_mlp, chips)),
        ],
        compiler_params=pltpu.CompilerParams(
            collective_id=0, has_side_effects=True, vmem_limit_bytes=room),
        name="gather_and_score",
    )(listing, listing, query_rows, key_rows, value_rows)
    return pl.pallas_call(
        finish_kernel,
        out_shape=jax.ShapeDtypeStruct((rows, heads * HD), jnp.bfloat16),
        in_specs=[anywhere, anywhere, whole, anywhere, anywhere, anywhere, anywhere],
        out_specs=anywhere,
        scratch_shapes=[
            pltpu.SMEM((q_blocks, kmax, H), jnp.int32),
            pltpu.SMEM((8, H), jnp.int32),
            pltpu.VMEM((half, rows, kmax * BLK), jnp.bfloat16),
            pltpu.VMEM((blocks, piece, width // 2), jnp.bfloat16),
            pltpu.VMEM((blocks, piece, width), jnp.bfloat16),
            pltpu.VMEM((rows, half * HD), jnp.bfloat16),
            pltpu.VMEM((rows, heads * HD), jnp.bfloat16),
            dma((5,)),
            dma((half,)),
            dma((heads,)),
        ],
        compiler_params=pltpu.CompilerParams(vmem_limit_bytes=room),
        name="attend_and_combine",
    )(listing, plan, kpos, probs, keys, values, query_rows)


def solution(mesh):
    placed = (
        P("seq", None),
        P(("seq", "mlp"), None),
        P(("seq", "mlp"), None),
        P(None, "seq", None),
    )
    return jax.shard_map(
        functools.partial(body, mesh.shape["seq"], mesh.shape["mlp"]),
        mesh=mesh, in_specs=placed, out_specs=P("seq", "mlp"), check_vma=False
    )
```
